32 devices in a mesh: grp: 2 (over y), reg: 16 (over z, x, core).
Axes of the slice: x: 2, y: 2, z: 4, core: 2. Of those that a mesh axis runs over, the one named last changes fastest.
Arguments:
- obs_value: float32 [512, 128, 256], P(('grp', 'reg')), parts along dimension 0, may hold values from -12 to 12
- positions: float32 [2, 512, 256], P(None, ('grp', 'reg')), parts along dimension 1, may hold values from 0 to 25
- sigma: float32 [512, 256], P(('grp', 'reg')), parts along dimension 0, may hold values from 0.5 to 2
- obs_var: float32 [512, 256], P(('grp', 'reg')), parts along dimension 0, may hold values from 0.3 to 3
- class_amp: float32 [3, 3], replicated, may hold values from 0.2 to 1
- length_scale: float32 [3], replicated, may hold values from 0.09 to 0.19
- block_class: int32 [512], P(('grp', 'reg')), parts along dimension 0, may hold values from 0 to 2
- block_count: int32 [32], P(('grp', 'reg')), parts along dimension 0, may hold values from 6 to 16, as said below
- pair_list: int32 [2, 1952], P(None, ('grp', 'reg')), parts along dimension 1, may hold values from 0 to 15, as said below
- pair_count: int32 [2, 32], P(None, ('grp', 'reg')), parts along dimension 1, may hold values from 0 to 46, as said below
Outputs:
- analysis_weights: float32 [512, 128, 256], P(('grp', 'reg')), parts along dimension 0
- residual: float32 [512, 128, 256], P(('grp', 'reg')), parts along dimension 0
The draws below stay inside these ranges and needn't reach their ends.
There are 2 independent parts, one for each index of `grp`. The reference program is written for one: setup_inputs(seed, part) draws one part's arguments, and reference() takes and returns one part's arrays. A program takes and returns all parts, laid end to end along the dimension named above; an argument that names none is the same for every part. Nothing has to cross between parts.
Inputs may be any that keep to these rules, and one draw needn't show every extreme that they name: `block_count`: A region's live blocks are its slots below its count; in every draw two neighbouring regions hold 16 live blocks. `pair_list`: listed pairs join live blocks only, each block pair at most once; within a region's 61 entries the pairs inside the region come first, then those with the next region, then unused entries. Some region fills all 61 entries in every draw. pair_count[0, r] + pair_count[1, r] <= 61; the last region has no pairs with a next region.
All inputs are finite; a program needn't handle non-finite values.
Results may differ from the reference program's by a relative error of at most 0.0003.
Values sent between devices are 32-bit elements; how exact they have to be, the bound alone decides.
A program may use at most 64 MiB of HBM per device.

```python
import math
import jax
import jax.numpy as jnp
from jax import lax

BS = 256
NCLS = 3
BLK = 16
NRHS = 128
ITERS = 2
PAIR_CAP = 61
BLOCKS = 256
N_REG = 16


def layout(key):
    key_band, key_count, key_cols, key_shift = jax.random.split(key, 4)
    column_span = 3 * BLK // 2
    far_column = 10 * column_span
    region_ids = jnp.arange(N_REG, dtype=jnp.int32)
    slot_ids = jnp.arange(BLK, dtype=jnp.int32)
    full_band = jax.random.randint(key_band, (), 0, N_REG - 1)
    counts = jax.random.randint(key_count, (N_REG,), 3 * BLK // 8, 7 * BLK // 8 + 1)
    is_full = (region_ids == full_band) | (region_ids == full_band + 1)
    counts = jnp.where(is_full, BLK, counts).astype(jnp.int32)
    live = slot_ids[None, :] < counts[:, None]
    shuffled = jax.vmap(lambda one_key: jax.random.permutation(one_key, column_span))(jax.random.split(key_cols, N_REG))[:, :BLK]
    columns = jnp.sort(jnp.where(live, shuffled, far_column), axis=1)
    start_col = jax.random.randint(key_shift, (), 0, column_span - BLK + 1)
    columns = jnp.where(is_full[:, None], start_col + slot_ids[None, :], columns).astype(jnp.int32)
    loc_ok = live[:, :-1] & live[:, 1:] & (columns[:, 1:] - columns[:, :-1] <= 1)
    north_cols = jnp.concatenate([columns[1:], jnp.full((1, BLK), far_column, jnp.int32)], axis=0)
    north_live = jnp.concatenate([live[1:], jnp.zeros((1, BLK), bool)], axis=0)
    cross_ok = live[:, :, None] & north_live[:, None, :] & (jnp.abs(columns[:, :, None] - north_cols[:, None, :]) <= 1)
    cross_ok = cross_ok.reshape(N_REG, BLK * BLK)
    loc_order = jnp.argsort((~loc_ok).astype(jnp.int32), axis=1, stable=True).astype(jnp.int32)
    cross_order = jnp.argsort((~cross_ok).astype(jnp.int32), axis=1, stable=True).astype(jnp.int32)
    loc_count = jnp.sum(loc_ok.astype(jnp.int32), axis=1)
    cross_count = jnp.sum(cross_ok.astype(jnp.int32), axis=1)
    entry_ids = jnp.arange(PAIR_CAP, dtype=jnp.int32)[None, :]
    in_loc = entry_ids < loc_count[:, None]
    in_cross = ~in_loc & (entry_ids < (loc_count + cross_count)[:, None])
    loc_pick = jnp.broadcast_to(jnp.minimum(entry_ids, BLK - 2), (N_REG, PAIR_CAP))
    cross_pick = jnp.clip(entry_ids - loc_count[:, None], 0, BLK * BLK - 1)
    loc_first = jnp.take_along_axis(loc_order, loc_pick, axis=1)
    cross_flat = jnp.take_along_axis(cross_order, cross_pick, axis=1)
    first_slot = jnp.where(in_loc, loc_first, jnp.where(in_cross, cross_flat // BLK, 0))
    second_slot = jnp.where(in_loc, loc_first + 1, jnp.where(in_cross, cross_flat % BLK, 0))
    pairs = jnp.stack([first_slot, second_slot]).reshape(2, N_REG * PAIR_CAP).astype(jnp.int32)
    pair_totals = jnp.stack([loc_count, cross_count]).astype(jnp.int32)
    return (counts, columns, live, pairs, pair_totals)


def draw_block_count(key, part):
    return layout(key)[0]


def draw_pair_list(key, part):
    return layout(key)[3]


def draw_pair_count(key, part):
    return layout(key)[4]


def draw_positions(key, part):
    counts, columns, live, pairs, pair_totals = layout(key)
    key = jax.random.fold_in(key, 5)
    key_east, key_north = jax.random.split(key)
    east_unit = jax.random.uniform(key_east, (N_REG, BLK, BS), jnp.float32)
    north_unit = jax.random.uniform(key_north, (N_REG, BLK, BS), jnp.float32)
    east_frac = east_unit
    north_frac = north_unit
    slot_ids = jnp.arange(BLK, dtype=jnp.int32)
    base_col = jnp.where(live, columns, slot_ids[None, :]).astype(jnp.float32)
    region_rows = jnp.arange(N_REG, dtype=jnp.int32).astype(jnp.float32)
    east_coord = base_col[:, :, None] + 0.2 + 1.6 * east_frac
    north_coord = region_rows[:, None, None] + 0.2 + 1.6 * north_frac
    return jnp.stack([east_coord, north_coord]).reshape(2, BLOCKS, BS)


def draw_obs_value(key, part):
    key = jax.random.fold_in(key, 7)
    region_frac = (jnp.arange(BLOCKS, dtype=jnp.int32) // BLK).astype(jnp.float32) / max(N_REG - 1, 1)
    noise = jnp.clip(jax.random.normal(key, (BLOCKS, NRHS, BS), jnp.float32), -4.0, 4.0)
    return noise * (3.0 ** region_frac)[:, None, None]


def with_ends(result, own_key, low, largest):
    dims = result.shape
    index_at = [jax.random.randint(jax.random.fold_in(own_key, axis), (), 0, dims[axis]) for axis in range(len(dims))]
    result = result.at[tuple(index_at)].set(low)
    longest = dims.index(max(dims))
    index_at[longest] = (index_at[longest] + 1) % dims[longest]
    return result.at[tuple(index_at)].set(largest)


def steps_of(rng, dims, cuts, smallest, top_value):
    loudness = 1.0
    for axis_at, shards_of in cuts:
        draws = jax.random.uniform(jax.random.fold_in(jax.random.fold_in(rng, 6), axis_at), (shards_of,), jnp.float32, smallest / len(cuts), top_value / len(cuts))
        loudness = loudness * jnp.repeat(jnp.exp(draws), dims[axis_at] // shards_of).reshape((-1,) + (1,) * (len(dims) - 1 - axis_at))
    return loudness


def setup_inputs(seed: int = 0, part: int = 0) -> dict:
    key_list = jax.random.split(jax.random.key(seed), 11)
    own_keys = jax.random.split(jax.random.fold_in(key_list[10], part), 11)
    return {
        "obs_value": draw_obs_value(jax.random.fold_in(jax.random.fold_in(key_list[10], part), 71), part),
        "positions": draw_positions(jax.random.fold_in(jax.random.fold_in(key_list[10], part), 71), part),
        "sigma": jnp.clip(jnp.exp(math.log(2.0) - 1.3862944 * jax.random.uniform(own_keys[2], (BLOCKS, BS), jnp.float32) ** steps_of(own_keys[2], (BLOCKS, BS), ((0, 16),), -0.2, 0.2)), 0.5, 2.0),
        "obs_var": jnp.clip(jnp.exp(math.log(3.0) - 2.3025851 * jax.random.uniform(own_keys[3], (BLOCKS, BS), jnp.float32) ** steps_of(own_keys[3], (BLOCKS, BS), ((0, 16),), -0.2, 0.2)), 0.3, 3.0),
        "class_amp": jnp.clip(jnp.exp(jax.random.uniform(key_list[4], (NCLS, NCLS), jnp.float32, math.log(0.2), math.log(1.0))), 0.2, 1.0),
        "length_scale": jnp.clip(jnp.exp(jax.random.uniform(key_list[5], (NCLS,), jnp.float32, math.log(0.09), math.log(0.19))), 0.09, 0.19),
        "block_class": with_ends(jax.random.randint(own_keys[6], (BLOCKS,), 0, NCLS), jax.random.fold_in(own_keys[6], 1), 0, NCLS - 1).astype(jnp.int32),
        "block_count": draw_block_count(jax.random.fold_in(jax.random.fold_in(key_list[10], part), 71), part),
        "pair_list": draw_pair_list(jax.random.fold_in(jax.random.fold_in(key_list[10], part), 71), part),
        "pair_count": draw_pair_count(jax.random.fold_in(jax.random.fold_in(key_list[10], part), 71), part),
    }


highest_precision = lax.Precision.HIGHEST

def gaspari(ratio):
    inner = (((-0.25 * ratio + 0.5) * ratio + 0.625) * ratio - 5.0 / 3.0) * ratio * ratio + 1.0
    safe_ratio = jnp.maximum(ratio, 1.0)
    outer = ((((ratio / 12.0 - 0.5) * ratio + 0.625) * ratio + 5.0 / 3.0) * ratio - 5.0) * ratio + 4.0 - 2.0 / (3.0 * safe_ratio)
    return jnp.where(ratio <= 1.0, inner, jnp.where(ratio <= 2.0, outer, jnp.zeros_like(ratio)))

def amplitude_rows(block_class, class_amp):
    class_ids = jnp.arange(class_amp.shape[0], dtype=jnp.int32)
    chosen = block_class[:, None, None] == class_ids[None, :, None]
    return lax.optimization_barrier(jnp.sum(jnp.where(chosen, class_amp[None, :, :], jnp.zeros_like(class_amp)[None]), axis=1))

def corr_tile(pos_first, pos_second, amp_first, amp_second, length_scale):
    east_gap = pos_first[0][:, None] - pos_second[0][None, :]
    north_gap = pos_first[1][:, None] - pos_second[1][None, :]
    distance = jnp.sqrt(east_gap * east_gap + north_gap * north_gap)
    running = jnp.zeros_like(distance)
    for cls_index in range(length_scale.shape[0]):
        running = running + amp_first[cls_index] * amp_second[cls_index] * gaspari(distance / length_scale[cls_index])
    return running

def reference(obs_value, positions, sigma, obs_var, class_amp, length_scale, block_class, block_count, pair_list, pair_count):
    amp_rows = amplitude_rows(block_class, class_amp)
    block_ids = jnp.arange(BLOCKS, dtype=jnp.int32)
    live_mask = (block_ids % BLK < block_count[block_ids // BLK]).astype(jnp.float32)
    pad_values = jnp.zeros((BLK, NRHS, BS), jnp.float32)
    pos_pad = jnp.concatenate([positions, jnp.zeros((2, BLK, BS), jnp.float32)], axis=1)
    amp_pad = jnp.concatenate([amp_rows, jnp.zeros((BLK, amp_rows.shape[1]), jnp.float32)], axis=0)
    pair_slots = jnp.arange(PAIR_CAP, dtype=jnp.int32)
    tiles_of = jax.vmap(corr_tile, in_axes=(1, 1, 0, 0, None))

    def operate(direction):
        scaled = sigma[:, None, :] * direction
        val_pad = jnp.concatenate([scaled, pad_values], axis=0)

        def region_step(spread, region):
            first_block = region * BLK
            values_two = lax.dynamic_slice_in_dim(val_pad, first_block, 2 * BLK, 0)
            pos_two = lax.dynamic_slice_in_dim(pos_pad, first_block, 2 * BLK, 1)
            amp_two = lax.dynamic_slice_in_dim(amp_pad, first_block, 2 * BLK, 0)
            diag_tiles = tiles_of(pos_two[:, :BLK], pos_two[:, :BLK], amp_two[:BLK], amp_two[:BLK], length_scale)
            diag_terms = jnp.einsum('bpq,bmq->bmp', diag_tiles, values_two[:BLK], precision=highest_precision)
            listed = lax.dynamic_slice_in_dim(pair_list, region * PAIR_CAP, PAIR_CAP, 1)
            local_count = pair_count[0, region]
            total_count = local_count + pair_count[1, region]
            first_rows = listed[0]
            second_rows = listed[1] + jnp.where(pair_slots >= local_count, BLK, 0).astype(jnp.int32)
            weight = (pair_slots < total_count).astype(jnp.float32)
            pair_tiles = tiles_of(pos_two[:, first_rows], pos_two[:, second_rows], amp_two[first_rows], amp_two[second_rows], length_scale)
            forward_terms = jnp.einsum('tpq,tmq->tmp', pair_tiles, values_two[second_rows], precision=highest_precision) * weight[:, None, None]
            backward_terms = jnp.einsum('tpq,tmp->tmq', pair_tiles, values_two[first_rows], precision=highest_precision) * weight[:, None, None]
            local_sum = jnp.zeros((2 * BLK, NRHS, BS), jnp.float32)
            local_sum = local_sum.at[:BLK].add(diag_terms)
            local_sum = local_sum.at[first_rows].add(forward_terms).at[second_rows].add(backward_terms)
            current = lax.dynamic_slice_in_dim(spread, first_block, 2 * BLK, 0)
            return (lax.dynamic_update_slice_in_dim(spread, current + local_sum, first_block, 0), None)
        spread, unused = lax.scan(region_step, jnp.zeros((BLOCKS + BLK, NRHS, BS), jnp.float32), jnp.arange(N_REG, dtype=jnp.int32))
        return sigma[:, None, :] * spread[:BLOCKS] + obs_var[:, None, :] * direction
    residual = obs_value * live_mask[:, None, None]
    weights = jnp.zeros_like(residual)
    direction = residual
    norm_now = lax.optimization_barrier(jnp.sum(residual * residual, axis=(0, 2)))
    for iteration in range(ITERS):
        applied = operate(direction)
        step_size = norm_now / lax.optimization_barrier(jnp.sum(direction * applied, axis=(0, 2)))
        weights = weights + step_size[None, :, None] * direction
        residual = residual - step_size[None, :, None] * applied
        if iteration + 1 < ITERS:
            norm_next = lax.optimization_barrier(jnp.sum(residual * residual, axis=(0, 2)))
            direction = residual + (norm_next / norm_now)[None, :, None] * direction
            norm_now = norm_next
    return (weights, residual)
```

```python
import functools

import jax
import jax.numpy as jnp
from jax import lax
from jax.experimental import pallas as pl
from jax.experimental.pallas import tpu as pltpu
from jax.sharding import PartitionSpec as P

SIDE_MAX = 46
SLOTS = 4
ROWS = 32
MESH = pl.DeviceIdType.MESH
VMEM_BYTES = 56 * 1024 * 1024
VMEM = pl.BlockSpec(memory_space=pltpu.VMEM)
SMEM = pl.BlockSpec(memory_space=pltpu.SMEM)
ANY = pl.BlockSpec(memory_space=pl.ANY)


def passed_along(shard, axis, by):
    length = lax.axis_size(axis)
    pairs = [(i, i + by) for i in range(length) if 0 <= i + by < length]
    return lax.ppermute(shard, axis, pairs)


def split_rows(values):
    high = values.astype(jnp.bfloat16)
    low = (values - high.astype(jnp.float32)).astype(jnp.bfloat16)
    return high, low


def product(stacked, tile_high, tile_low, contract):
    members = stacked.shape[0] // 2
    dims = (((1,), (contract,)), ((), ()))
    first = lax.dot_general(stacked, tile_high, dims, preferred_element_type=jnp.float32)
    second = lax.dot_general(
        stacked[:members], tile_low, dims, preferred_element_type=jnp.float32
    )
    return first[:members] + first[members:] + second


def build_tile(pos_src, src, pos_dst, dst, cls_src, cls_dst, amp_ref, scale_ref, tile_ref):
    size = pos_dst.shape[2]
    columns = [
        jnp.transpose(jnp.broadcast_to(pos_src[axis, pl.ds(src, 1), :], (8, size)))
        for axis in range(2)
    ]
    rows = [pos_dst[axis, pl.ds(dst, 1), :] for axis in range(2)]
    classes = []
    for k in range(amp_ref.shape[1]):
        weight = amp_ref[cls_src, k] * amp_ref[cls_dst, k]
        scale = scale_ref[0, k]
        inv = scale_ref[1, k]
        inv2 = inv * inv
        classes.append(
            (
                scale,
                2.0 * scale,
                -0.5 * scale * scale,
                weight * inv2 * inv2 * inv * (1.0 / 12.0),
                weight,
                weight * inv2 * (-5.0 / 3.0),
                weight * inv2 * inv * 0.625,
                weight * inv2 * inv2 * 0.5,
                weight * inv2 * inv2 * inv * -0.25,
            )
        )
    for start in range(0, size, ROWS):
        part = slice(start, start + ROWS)
        east = columns[0][part, :1] - rows[0]
        north = columns[1][part, :1] - rows[1]
        square = east * east + north * north
        inverse = lax.rsqrt(jnp.maximum(square, 1e-30))
        dist = square * inverse
        total = None
        for scale, twice, shift, out_w, c0, c2, c3, c4, c5 in classes:
            inner = c0 + square * (c2 + dist * (c3 + dist * (c4 + dist * c5)))
            gap = jnp.maximum(twice - dist, 0.0)
            gap = gap * gap
            outer = (gap * gap) * ((square + dist * twice + shift) * (inverse * out_w))
            term = jnp.where(dist <= scale, inner, outer)
            total = term if total is None else total + term
        high, low = split_rows(total)
        tile_ref[0, part, :] = high
        tile_ref[1, part, :] = low


def tile_loop(build, base, count, tiles_ref, slots, sems, make, use):
    def copy(t):
        slot = lax.rem(t, SLOTS)
        if build:
            return pltpu.make_async_copy(slots.at[slot], tiles_ref.at[base + t], sems.at[slot])
        return pltpu.make_async_copy(tiles_ref.at[base + t], slots.at[slot], sems.at[slot])

    if build:

        def step(t, carry):
            slot = lax.rem(t, SLOTS)

            @pl.when(t >= SLOTS)
            def _():
                copy(t - SLOTS).wait()

            make(t, slots.at[slot])
            copy(t).start()
            use(t, slots.at[slot])
            return carry

        lax.fori_loop(0, count, step, 0)

        def drain(t, carry):
            copy(t).wait()
            return carry

        lax.fori_loop(jnp.maximum(count - SLOTS, 0), count, drain, 0)
    else:

        def warm(t, carry):
            copy(t).start()
            return carry

        lax.fori_loop(0, jnp.minimum(count, SLOTS - 1), warm, 0)

        def step(t, carry):
            @pl.when(t + SLOTS - 1 < count)
            def _():
                copy(t + SLOTS - 1).start()

            copy(t).wait()
            use(t, slots.at[lax.rem(t, SLOTS)])
            return carry

        lax.fori_loop(0, count, step, 0)


def stage_values(values, stacked):
    for start, blocks, block_of in values:

        def step(b, carry):
            members = stacked.shape[1] // 2
            high, low = split_rows(block_of(b))
            stacked[start + b, :members, :] = high
            stacked[start + b, members:, :] = low
            return carry

        lax.fori_loop(0, blocks, step, 0)


def mixed(coef_ref, base_ref, image_ref):
    if coef_ref is None:
        return lambda b: base_ref[b]

    def block(b):
        keep = jnp.concatenate([coef_ref[0], coef_ref[0]], axis=1)
        take = jnp.concatenate([coef_ref[1], coef_ref[1]], axis=1)
        return keep * base_ref[b] - take * image_ref[b]

    return block


def own_kernel(build, entries, *refs):
    if build:
        info, amp, scale, pos, base, tiles, acc, stacked, slots, sems = refs
        coef = image = None
    else:
        info, coef, base, image, tiles, acc, stacked, slots, sems = refs
    local_pairs = info[2 * entries]
    live = info[2 * entries + 2]
    blocks = base.shape[0]
    acc[...] = jnp.zeros_like(acc)
    stage_values([(0, blocks, mixed(coef, base, image))], stacked)

    def ends(t):
        entry = jnp.clip(t - live, 0, entries - 1)
        src = jnp.where(t < live, t, info[entry])
        dst = jnp.where(t < live, t, info[entries + entry])
        return src, dst

    def make(t, tile):
        src, dst = ends(t)
        first = 2 * entries + 3
        build_tile(pos, src, pos, dst, info[first + src], info[first + dst], amp, scale, tile)

    def use(t, tile):
        src, dst = ends(t)
        acc[dst] += product(stacked[src], tile[0], tile[1], 0)

        @pl.when(t >= live)
        def _():
            acc[src] += product(stacked[dst], tile[0], tile[1], 1)

    tile_loop(build, 0, live + local_pairs, tiles, slots, sems, make, use)


def cross_kernel(build, entries, *refs):
    if build:
        (info, info_n, info_s, amp, scale, pos, pos_two, base_n, base_s, acc_in, sigma, obs_var,
         direct, tiles_in, tiles, image_out, scaled_out, sums, stacked, slots, sems, parts) = refs
        coef = image_n = image_s = image = None
    else:
        (info, info_n, info_s, coef, base_n, image_n, base_s, image_s, acc_in, sigma, obs_var,
         direct, image, tiles, image_out, sums, stacked, slots, sems, parts) = refs
    blocks = acc_in.shape[0]
    local_pairs = info[2 * entries]
    north_pairs = info[2 * entries + 1]
    local_south = info_s[2 * entries]
    south_pairs = info_s[2 * entries + 1]
    image_out[...] = acc_in[...]
    stage_values(
        [
            (0, blocks, mixed(coef, base_n, image_n)),
            (blocks, blocks, mixed(coef, base_s, image_s)),
        ],
        stacked,
    )

    def ends(t):
        is_north = t < north_pairs
        entry_n = jnp.clip(local_pairs + t, 0, entries - 1)
        entry_s = jnp.clip(local_south + t - north_pairs, 0, entries - 1)
        far_n = info[entries + entry_n]
        far_s = info_s[entry_s]
        dst = jnp.where(is_north, info[entry_n], info_s[entries + entry_s])
        return is_north, far_n, far_s, dst

    def make(t, tile):
        is_north, far_n, far_s, dst = ends(t)
        first = 2 * entries + 3
        src = jnp.where(is_north, far_n, blocks + far_s)
        cls_src = jnp.where(is_north, info_n[first + far_n], info_s[first + far_s])
        build_tile(pos_two, src, pos, dst, cls_src, info[first + dst], amp, scale, tile)

    def use(t, tile):
        is_north, far_n, far_s, dst = ends(t)
        src = jnp.where(is_north, far_n, blocks + far_s)
        image_out[dst] += product(stacked[src], tile[0], tile[1], 0)

    before = info[2 * entries + 2] + local_pairs
    tile_loop(build, before, north_pairs + south_pairs, tiles, slots, sems, make, use)

    parts[...] = jnp.zeros_like(parts)
    direction_of = mixed(coef, direct, image)
    half = parts.shape[2]

    def finish(b, carry):
        weight = sigma[pl.ds(b, 1), :]
        direction = direction_of(b)
        result = weight * image_out[b] + obs_var[pl.ds(b, 1), :] * direction
        image_out[b] = result
        if build:
            scaled_out[b] = weight * result
        terms = [direction * result]
        if build:
            terms += [direction * direction, result * result]
        for k, term in enumerate(terms):
            parts[k] += term[:, :half] + term[:, half:]
        return carry

    lax.fori_loop(0, blocks, finish, 0)
    sums[...] = jnp.zeros_like(sums)
    for k in range(3 if build else 1):
        sums[k : k + 1, :] = jnp.sum(jnp.transpose(parts[k]), axis=0, keepdims=True)


def total_kernel(n, value, out, held, send_sems, recv_sems):
    me = lax.axis_index("reg")
    stages = n.bit_length() - 1
    barrier = pltpu.get_barrier_semaphore()

    def partner(stage):
        step = 1 << stage
        upper = lax.rem(lax.div(me, step), 2)
        return me + step - 2 * step * upper

    for stage in range(stages):
        pl.semaphore_signal(
            barrier, inc=1, device_id={"reg": partner(stage)}, device_id_type=MESH
        )
    pl.semaphore_wait(barrier, stages)
    held[0] = value[...]
    for stage in range(stages):
        copy = pltpu.make_async_remote_copy(
            src_ref=held.at[2 * stage],
            dst_ref=held.at[2 * stage + 1],
            send_sem=send_sems.at[stage],
            recv_sem=recv_sems.at[stage],
            device_id={"reg": partner(stage)},
            device_id_type=MESH,
        )
        copy.start()
        copy.wait()
        held[2 * stage + 2] = held[2 * stage] + held[2 * stage + 1]
    out[...] = held[2 * stages]


def total_over(value, call):
    n = lax.axis_size("reg")
    if n & (n - 1):
        return lax.psum(value, "reg")
    stages = n.bit_length() - 1
    return pl.pallas_call(
        functools.partial(total_kernel, n),
        out_shape=jax.ShapeDtypeStruct(value.shape, value.dtype),
        in_specs=[VMEM],
        out_specs=VMEM,
        scratch_shapes=[
            pltpu.VMEM((2 * stages + 1,) + value.shape, value.dtype),
            pltpu.SemaphoreType.DMA((stages,)),
            pltpu.SemaphoreType.DMA((stages,)),
        ],
        compiler_params=pltpu.CompilerParams(collective_id=call, has_side_effects=True),
        name="member_sums_%d" % call,
    )(value)


def local(
    obs_value,
    positions,
    sigma,
    obs_var,
    class_amp,
    length_scale,
    block_class,
    block_count,
    pair_list,
    pair_count,
):
    blocks, members, size = obs_value.shape
    entries = pair_list.shape[1]
    info = jnp.concatenate(
        [pair_list[0], pair_list[1], pair_count[:, 0], block_count, block_class]
    )
    width = info.shape[0]
    packed = jnp.concatenate(
        [
            positions.reshape(2 * blocks, size),
            jnp.pad(info.astype(jnp.float32), (0, -width % size)).reshape(-1, size),
        ]
    )
    packed_n = passed_along(packed, "reg", -1)
    packed_s = passed_along(packed, "reg", 1)
    pos_n, pos_s = (p[: 2 * blocks].reshape(2, blocks, size) for p in (packed_n, packed_s))
    info_n, info_s = (
        p[2 * blocks :].reshape(-1)[:width].astype(jnp.int32) for p in (packed_n, packed_s)
    )
    pos_two = jnp.concatenate([pos_n, pos_s], axis=1)
    scales = jnp.stack([length_scale, 1.0 / length_scale])

    live = (jnp.arange(blocks, dtype=jnp.int32) < block_count[0]).astype(jnp.float32)
    first_residual = obs_value * live[:, None, None]
    scaled = sigma[:, None, :] * first_residual
    scaled_n = passed_along(scaled, "reg", -1)
    scaled_s = passed_along(scaled, "reg", 1)

    own_cap = blocks + min(SIDE_MAX, entries)
    cross_cap = 2 * min(SIDE_MAX, entries)
    cap = blocks + entries + min(SIDE_MAX, entries)
    array = jax.ShapeDtypeStruct((blocks, members, size), jnp.float32)
    sums_shape = jax.ShapeDtypeStruct((8, members), jnp.float32)

    tiles_shape = jax.ShapeDtypeStruct((cap, 2, size, size), jnp.bfloat16)

    def scratch(count):
        return [
            pltpu.VMEM((count, 2 * members, size), jnp.bfloat16),
            pltpu.VMEM((SLOTS, 2, size, size), jnp.bfloat16),
            pltpu.SemaphoreType.DMA((SLOTS,)),
        ]

    parts = [pltpu.VMEM((3, members, size // 2), jnp.float32)]
    params = pltpu.CompilerParams(vmem_limit_bytes=VMEM_BYTES)

    def cost(count, build):
        return pl.CostEstimate(
            flops=count * 6 * size * size * members + build * count * 80 * size * size,
            bytes_accessed=count * 4 * size * size,
            transcendentals=build * count * size * size,
        )

    tiles, spread = pl.pallas_call(
        functools.partial(own_kernel, True, entries),
        out_shape=[tiles_shape, array],
        in_specs=[SMEM, SMEM, SMEM, VMEM, VMEM],
        out_specs=[ANY, VMEM],
        scratch_shapes=scratch(blocks),
        compiler_params=params,
        cost_estimate=cost(own_cap, 1),
        name="own_tiles_and_spread",
    )(info, class_amp, scales, positions, scaled)
    tiles, image, scaled_image, sums = pl.pallas_call(
        functools.partial(cross_kernel, True, entries),
        out_shape=[tiles_shape, array, array, sums_shape],
        in_specs=[SMEM] * 5 + [VMEM] * 8 + [ANY],
        out_specs=[ANY, VMEM, VMEM, VMEM],
        input_output_aliases={13: 0},
        scratch_shapes=scratch(2 * blocks) + parts,
        compiler_params=params,
        cost_estimate=cost(cross_cap, 1),
        name="cross_tiles_and_image",
    )(
        info, info_n, info_s, class_amp, scales, positions, pos_two, scaled_n, scaled_s, spread,
        sigma, obs_var, first_residual, tiles,
    )
    image_n = passed_along(scaled_image, "reg", -1)
    image_s = passed_along(scaled_image, "reg", 1)
    totals = total_over(sums, 0)
    curvature, norm = totals[0], totals[1]
    step = norm / curvature
    norm_next = jnp.maximum(norm - 2.0 * step * curvature + step * step * totals[2], 0.0)
    keep = 1.0 + norm_next / norm
    coef = jnp.broadcast_to(jnp.stack([keep, step])[:, :, None], (2, members, size // 2))

    spread = pl.pallas_call(
        functools.partial(own_kernel, False, entries),
        out_shape=array,
        in_specs=[SMEM, VMEM, VMEM, VMEM, ANY],
        out_specs=VMEM,
        scratch_shapes=scratch(blocks),
        compiler_params=params,
        cost_estimate=cost(own_cap, 0),
        name="own_spread",
    )(info, coef, scaled, scaled_image, tiles)
    image_two, sums = pl.pallas_call(
        functools.partial(cross_kernel, False, entries),
        out_shape=[array, sums_shape],
        in_specs=[SMEM] * 3 + [VMEM] * 10 + [ANY],
        out_specs=[VMEM, VMEM],
        scratch_shapes=scratch(2 * blocks) + parts,
        compiler_params=params,
        cost_estimate=cost(cross_cap, 0),
        name="cross_image",
    )(
        info, info_n, info_s, coef, scaled_n, image_n, scaled_s, image_s, spread, sigma, obs_var,
        first_residual, image, tiles,
    )
    step_two = norm_next / total_over(sums, 1)[0]
    along = lambda member_values: member_values[None, :, None]
    direction_two = along(keep) * first_residual - along(step) * image
    weights = along(step) * first_residual + along(step_two) * direction_two
    residual = first_residual - along(step) * image - along(step_two) * image_two
    return (weights, residual)


def solution(mesh):
    placed = (
        P(("grp", "reg"), None, None),
        P(None, ("grp", "reg"), None),
        P(("grp", "reg"), None),
        P(("grp", "reg"), None),
        P(),
        P(),
        P(("grp", "reg")),
        P(("grp", "reg")),
        P(None, ("grp", "reg")),
        P(None, ("grp", "reg")),
    )
    return jax.shard_map(
        local,
        mesh=mesh,
        in_specs=placed,
        out_specs=(P(("grp", "reg"), None, None), P(("grp", "reg"), None, None)),
        check_vma=False,
    )
```

```python
import functools

import jax
import jax.numpy as jnp
from jax import lax
from jax.experimental import pallas as pl
from jax.experimental.pallas import tpu as pltpu
from jax.sharding import PartitionSpec as P

SIDE_MAX = 46
SLOTS = 4
GROUP = 4
ROWS = 16
MESH = pl.DeviceIdType.MESH
VMEM_BYTES = 56 * 1024 * 1024
VMEM = pl.BlockSpec(memory_space=pltpu.VMEM)
SMEM = pl.BlockSpec(memory_space=pltpu.SMEM)
ANY = pl.BlockSpec(memory_space=pl.ANY)


def passed_along(shard, axis, by):
    length = lax.axis_size(axis)
    pairs = [(i, i + by) for i in range(length) if 0 <= i + by < length]
    return lax.ppermute(shard, axis, pairs)


def split_rows(values):
    high = values.astype(jnp.bfloat16)
    low = (values - high.astype(jnp.float32)).astype(jnp.bfloat16)
    return high, low


def product(stacked, tile_high, tile_low, contract):
    members = stacked.shape[0] // 2
    dims = (((1,), (contract,)), ((), ()))
    first = lax.dot_general(stacked, tile_high, dims, preferred_element_type=jnp.float32)
    second = lax.dot_general(
        stacked[:members], tile_low, dims, preferred_element_type=jnp.float32
    )
    return first[:members] + first[members:] + second


def build_tile(pos_src, src, pos_dst, dst, cls_src, cls_dst, amp_ref, scale_ref, tile_ref):
    size = pos_dst.shape[2]
    columns = [
        jnp.transpose(jnp.broadcast_to(pos_src[axis, pl.ds(src, 1), :], (8, size)))
        for axis in range(2)
    ]
    rows = [pos_dst[axis, pl.ds(dst, 1), :] for axis in range(2)]
    classes = []
    for k in range(amp_ref.shape[1]):
        weight = amp_ref[cls_src, k] * amp_ref[cls_dst, k]
        scale = scale_ref[0, k]
        inv = scale_ref[1, k]
        inv2 = inv * inv
        classes.append(
            (
                scale,
                2.0 * scale,
                -0.5 * scale * scale,
                weight * inv2 * inv2 * inv * (1.0 / 12.0),
                weight,
                weight * inv2 * (-5.0 / 3.0),
                weight * inv2 * inv * 0.625,
                weight * inv2 * inv2 * 0.5,
                weight * inv2 * inv2 * inv * -0.25,
            )
        )
    for start in range(0, size, ROWS):
        part = slice(start, start + ROWS)
        east = columns[0][part, :1] - rows[0]
        north = columns[1][part, :1] - rows[1]
        square = east * east + north * north
        inverse = lax.rsqrt(jnp.maximum(square, 1e-30))
        dist = square * inverse
        total = None
        for scale, twice, shift, out_w, c0, c2, c3, c4, c5 in classes:
            inner = c0 + square * (c2 + dist * (c3 + dist * (c4 + dist * c5)))
            gap = jnp.maximum(twice - dist, 0.0)
            gap = gap * gap
            outer = (gap * gap) * ((square + dist * twice + shift) * (inverse * out_w))
            term = jnp.where(dist <= scale, inner, outer)
            total = term if total is None else total + term
        high, low = split_rows(total)
        tile_ref[0, part, :] = high
        tile_ref[1, part, :] = low


def build_loop(base, count, tiles_ref, slots, sems, make, use):
    def slot_of(t):
        return slots.at[lax.rem(t, SLOTS)]

    def copy(t):
        return pltpu.make_async_copy(slot_of(t), tiles_ref.at[base + t], sems.at[lax.rem(t, SLOTS)])

    @pl.when(count > 0)
    def _():
        make(0, slots.at[0])
        copy(0).start()

    def step(t, carry):
        @pl.when(t >= SLOTS)
        def _():
            copy(t - SLOTS).wait()

        use([(t - 1, slot_of(t - 1))])
        make(t, slot_of(t))
        copy(t).start()
        return carry

    lax.fori_loop(1, count, step, 0)

    @pl.when(count > 0)
    def _():
        use([(count - 1, slot_of(count - 1))])

    def drain(t, carry):
        copy(t).wait()
        return carry

    lax.fori_loop(jnp.maximum(count - SLOTS, 0), count, drain, 0)


def read_loop(base, count, tiles_ref, slots, sems, use):
    groups = lax.div(count + GROUP - 1, GROUP)

    def copy(g):
        slot = lax.rem(g, 2)
        return pltpu.make_async_copy(
            tiles_ref.at[pl.ds(base + g * GROUP, GROUP)], slots.at[slot], sems.at[slot]
        )

    @pl.when(groups > 0)
    def _():
        copy(0).start()

    def step(g, carry):
        @pl.when(g + 1 < groups)
        def _():
            copy(g + 1).start()

        copy(g).wait()
        use([(g * GROUP + j, slots.at[lax.rem(g, 2), j]) for j in range(GROUP)])
        return carry

    lax.fori_loop(0, groups, step, 0)


def stage_values(start, count, base_ref, stacked):
    members = stacked.shape[1] // 2

    def step(b, carry):
        high, low = split_rows(base_ref[b])
        stacked[start + b, :members, :] = high
        stacked[start + b, members:, :] = low
        return carry

    lax.fori_loop(0, count, step, 0)


def add_all(acc, terms):
    for where, term in terms:
        acc[where] += term


def own_kernel(build, entries, *refs):
    if build:
        info, amp, scale, pos, base, tiles, acc, stacked, slots, sems = refs
    else:
        info, base, tiles, acc, stacked, slots, sems = refs
    live = info[2 * entries + 2]
    count = live + info[2 * entries]
    blocks = stacked.shape[0]
    acc[...] = jnp.zeros_like(acc)
    stage_values(0, blocks, base, stacked)

    def ends(t):
        entry = jnp.clip(t - live, 0, entries - 1)
        src = jnp.where(t < live, t, info[entry])
        dst = jnp.where(t < live, t, info[entries + entry])
        return src, dst

    def make(t, tile):
        src, dst = ends(t)
        first = 2 * entries + 3
        build_tile(pos, src, pos, dst, info[first + src], info[first + dst], amp, scale, tile)

    def use(items):
        terms = []
        for t, tile in items:
            src, dst = ends(t)
            to = jnp.where(t < count, dst, blocks)
            back = jnp.where(jnp.logical_and(t >= live, t < count), src, blocks)
            terms.append((to, product(stacked[src], tile[0], tile[1], 0)))
            terms.append((back, product(stacked[dst], tile[0], tile[1], 1)))
        add_all(acc, terms)

    if build:
        build_loop(0, count, tiles, slots, sems, make, use)
    else:
        read_loop(0, count, tiles, slots, sems, use)


def cross_kernel(build, entries, *refs):
    if build:
        (info, info_n, info_s, amp, scale, pos, pos_two, base_n, base_s, acc_in, sigma, obs_var,
         direct, tiles_in, tiles, image_out, scaled_out, sums, stacked, slots, sems, acc, parts) = refs
    else:
        (info, info_n, info_s, base_n, base_s, acc_in, sigma, obs_var,
         direct, sums_in, tiles, image_out, sums, stacked, slots, sems, acc, parts) = refs
    blocks = image_out.shape[0]
    local_pairs = info[2 * entries]
    north_pairs = info[2 * entries + 1]
    local_south = info_s[2 * entries]
    south_pairs = info_s[2 * entries + 1]
    count = north_pairs + south_pairs
    acc[...] = acc_in[...]
    stage_values(0, blocks, base_n, stacked)
    stage_values(blocks, blocks, base_s, stacked)

    def ends(t):
        is_north = t < north_pairs
        entry_n = jnp.clip(local_pairs + t, 0, entries - 1)
        entry_s = jnp.clip(local_south + t - north_pairs, 0, entries - 1)
        far_n = info[entries + entry_n]
        far_s = info_s[entry_s]
        dst = jnp.where(is_north, info[entry_n], info_s[entries + entry_s])
        return is_north, far_n, far_s, dst

    def make(t, tile):
        is_north, far_n, far_s, dst = ends(t)
        first = 2 * entries + 3
        src = jnp.where(is_north, far_n, blocks + far_s)
        cls_src = jnp.where(is_north, info_n[first + far_n], info_s[first + far_s])
        build_tile(pos_two, src, pos, dst, cls_src, info[first + dst], amp, scale, tile)

    def use(items):
        terms = []
        for t, tile in items:
            is_north, far_n, far_s, dst = ends(t)
            src = jnp.where(is_north, far_n, blocks + far_s)
            to = jnp.where(t < count, dst, blocks)
            terms.append((to, product(stacked[src], tile[0], tile[1], 0)))
        add_all(acc, terms)

    before = info[2 * entries + 2] + local_pairs
    if build:
        build_loop(before, count, tiles, slots, sems, make, use)
    else:
        read_loop(before, count, tiles, slots, sems, use)

    parts[...] = jnp.zeros_like(parts)
    half = parts.shape[2]

    def finish(b, carry):
        weight = sigma[pl.ds(b, 1), :]
        direction = direct[b]
        result = weight * acc[b] + obs_var[pl.ds(b, 1), :] * direction
        image_out[b] = result
        if build:
            scaled_out[b] = weight * result
        terms = [direction * result]
        if build:
            terms += [direction * direction, result * result]
        for k, term in enumerate(terms):
            parts[k] += term[:, :half] + term[:, half:]
        return carry

    lax.fori_loop(0, blocks, finish, 0)
    if build:
        sums[...] = jnp.zeros_like(sums)
    else:
        sums[...] = sums_in[...]
    for k in range(3 if build else 1):
        row = k if build else 3
        sums[row : row + 1, :] = jnp.sum(jnp.transpose(parts[k]), axis=0, keepdims=True)


def total_kernel(low, high, value, out, held_low, held_high, send_low, recv_low, send_high, recv_high):
    me = lax.axis_index("reg")
    place_low, place_high = lax.rem(me, low), lax.div(me, low)

    def peer(stage, k):
        if stage == 0:
            return me - place_low + lax.rem(place_low + k, low)
        return lax.rem(place_high + k, high) * low + place_low

    barrier = pltpu.get_barrier_semaphore()
    for stage, size in enumerate((low, high)):
        for k in range(1, size):
            pl.semaphore_signal(
                barrier, inc=1, device_id={"reg": peer(stage, k)}, device_id_type=MESH
            )
    pl.semaphore_wait(barrier, low + high - 2)
    running = value[...]
    for stage, size, place, held, send, recv in (
        (0, low, place_low, held_low, send_low, recv_low),
        (1, high, place_high, held_high, send_high, recv_high),
    ):
        held[0] = running
        copies = []
        for k in range(1, size):
            copy = pltpu.make_async_remote_copy(
                src_ref=held.at[0],
                dst_ref=held.at[k],
                send_sem=send.at[k],
                recv_sem=recv.at[k],
                device_id={"reg": peer(stage, k)},
                device_id_type=MESH,
            )
            copy.start()
            copies.append(copy)
        for copy in copies:
            copy.wait()
        running = held[lax.rem(place, size)]
        for source in range(1, size):
            running = running + held[lax.rem(place - source + size, size)]
    out[...] = running


def total_over(value):
    n = lax.axis_size("reg")
    if n & (n - 1) or n < 4:
        return lax.psum(value, "reg")
    low = 1 << ((n.bit_length() - 1) // 2)
    high = n // low
    semaphores = [
        pltpu.SemaphoreType.DMA((size,)) for size in (low, low, high, high)
    ]
    return pl.pallas_call(
        functools.partial(total_kernel, low, high),
        out_shape=jax.ShapeDtypeStruct(value.shape, value.dtype),
        in_specs=[VMEM],
        out_specs=VMEM,
        scratch_shapes=[
            pltpu.VMEM((low,) + value.shape, value.dtype),
            pltpu.VMEM((high,) + value.shape, value.dtype),
        ]
        + semaphores,
        compiler_params=pltpu.CompilerParams(collective_id=0, has_side_effects=True),
        name="member_sums",
    )(value)


def local(
    obs_value,
    positions,
    sigma,
    obs_var,
    class_amp,
    length_scale,
    block_class,
    block_count,
    pair_list,
    pair_count,
):
    blocks, members, size = obs_value.shape
    entries = pair_list.shape[1]
    info = jnp.concatenate(
        [pair_list[0], pair_list[1], pair_count[:, 0], block_count, block_class]
    )
    width = info.shape[0]
    info_rows = -(-width // size)
    packed = jnp.concatenate(
        [
            positions.reshape(2 * blocks, size),
            jnp.pad(info.astype(jnp.float32), (0, -width % size)).reshape(-1, size),
        ]
    )
    packed = jnp.pad(packed, ((0, -packed.shape[0] % members), (0, 0)))
    packed = packed.reshape(-1, members, size)
    scales = jnp.stack([length_scale, 1.0 / length_scale])

    live = (jnp.arange(blocks, dtype=jnp.int32) < block_count[0]).astype(jnp.float32)
    first_residual = obs_value * live[:, None, None]
    scaled = jnp.concatenate([sigma[:, None, :] * first_residual, packed])
    scaled_n = passed_along(scaled, "reg", -1)
    scaled_s = passed_along(scaled, "reg", 1)

    def unpacked(bundle):
        rows = bundle[blocks:].reshape(-1, size)
        listed = rows[2 * blocks : 2 * blocks + info_rows].reshape(-1)[:width]
        return rows[: 2 * blocks].reshape(2, blocks, size), listed.astype(jnp.int32)

    pos_n, info_n = unpacked(scaled_n)
    pos_s, info_s = unpacked(scaled_s)
    pos_two = jnp.concatenate([pos_n, pos_s], axis=1)

    own_cap = blocks + min(SIDE_MAX, entries)
    cross_cap = 2 * min(SIDE_MAX, entries)
    cap = blocks + entries + min(SIDE_MAX, entries) + GROUP - 1
    array = jax.ShapeDtypeStruct((blocks, members, size), jnp.float32)
    spread_shape = jax.ShapeDtypeStruct((blocks + 1, members, size), jnp.float32)
    sums_shape = jax.ShapeDtypeStruct((8, members), jnp.float32)
    tiles_shape = jax.ShapeDtypeStruct((cap, 2, size, size), jnp.bfloat16)

    def scratch(count, build):
        held = (SLOTS,) if build else (2, GROUP)
        return [
            pltpu.VMEM((count, 2 * members, size), jnp.bfloat16),
            pltpu.VMEM(held + (2, size, size), jnp.bfloat16),
            pltpu.SemaphoreType.DMA((SLOTS if build else 2,)),
        ]

    parts = [
        pltpu.VMEM(spread_shape.shape, jnp.float32),
        pltpu.VMEM((3, members, size // 2), jnp.float32),
    ]
    params = pltpu.CompilerParams(vmem_limit_bytes=VMEM_BYTES)

    def cost(count, build):
        return pl.CostEstimate(
            flops=count * 6 * size * size * members + build * count * 80 * size * size,
            bytes_accessed=count * 4 * size * size,
            transcendentals=build * count * size * size,
        )

    tiles, spread = pl.pallas_call(
        functools.partial(own_kernel, True, entries),
        out_shape=[tiles_shape, spread_shape],
        in_specs=[SMEM, SMEM, SMEM, VMEM, VMEM],
        out_specs=[ANY, VMEM],
        scratch_shapes=scratch(blocks, True),
        compiler_params=params,
        cost_estimate=cost(own_cap, 1),
        name="own_tiles_and_spread",
    )(info, class_amp, scales, positions, scaled)
    tiles, image, scaled_image, sums = pl.pallas_call(
        functools.partial(cross_kernel, True, entries),
        out_shape=[tiles_shape, array, array, sums_shape],
        in_specs=[SMEM] * 5 + [VMEM] * 8 + [ANY],
        out_specs=[ANY, VMEM, VMEM, VMEM],
        input_output_aliases={13: 0},
        scratch_shapes=scratch(2 * blocks, True) + parts,
        compiler_params=params,
        cost_estimate=cost(cross_cap, 1),
        name="cross_tiles_and_image",
    )(
        info, info_n, info_s, class_amp, scales, positions, pos_two, scaled_n, scaled_s, spread,
        sigma, obs_var, first_residual, tiles,
    )
    image_n = passed_along(scaled_image, "reg", -1)
    image_s = passed_along(scaled_image, "reg", 1)
    spread = pl.pallas_call(
        functools.partial(own_kernel, False, entries),
        out_shape=spread_shape,
        in_specs=[SMEM, VMEM, ANY],
        out_specs=VMEM,
        scratch_shapes=scratch(blocks, False),
        compiler_params=params,
        cost_estimate=cost(own_cap, 0),
        name="own_spread",
    )(info, scaled_image, tiles)
    second_image, sums = pl.pallas_call(
        functools.partial(cross_kernel, False, entries),
        out_shape=[array, sums_shape],
        in_specs=[SMEM] * 3 + [VMEM] * 7 + [ANY],
        out_specs=[VMEM, VMEM],
        scratch_shapes=scratch(2 * blocks, False) + parts,
        compiler_params=params,
        cost_estimate=cost(cross_cap, 0),
        name="cross_image",
    )(info, info_n, info_s, image_n, image_s, spread, sigma, obs_var, image, sums, tiles)

    totals = total_over(sums)
    curvature, norm = totals[0], totals[1]
    step = norm / curvature
    norm_next = jnp.maximum(norm - 2.0 * step * curvature + step * step * totals[2], 0.0)
    keep = 1.0 + norm_next / norm
    curvature_next = keep * (keep * curvature - 2.0 * step * totals[2]) + step * step * totals[3]
    step_next = norm_next / curvature_next

    def along(member_values):
        return member_values[None, :, None]

    weights = along(step + step_next * keep) * first_residual - along(step_next * step) * image
    residual = (
        first_residual
        - along(step + step_next * keep) * image
        + along(step_next * step) * second_image
    )
    return (weights, residual)


def solution(mesh):
    placed = (
        P(("grp", "reg"), None, None),
        P(None, ("grp", "reg"), None),
        P(("grp", "reg"), None),
        P(("grp", "reg"), None),
        P(),
        P(),
        P(("grp", "reg")),
        P(("grp", "reg")),
        P(None, ("grp", "reg")),
        P(None, ("grp", "reg")),
    )
    return jax.shard_map(
        local,
        mesh=mesh,
        in_specs=placed,
        out_specs=(P(("grp", "reg"), None, None), P(("grp", "reg"), None, None)),
        check_vma=False,
    )
```

```python
import functools

import jax
import jax.numpy as jnp
from jax import lax
from jax.experimental import pallas as pl
from jax.experimental.pallas import tpu as pltpu
from jax.sharding import PartitionSpec as P

SIDE_MAX = 46
SLOTS = 4
GROUP = 4
ROWS = 16
MESH = pl.DeviceIdType.MESH
VMEM_BYTES = 56 * 1024 * 1024
VMEM = pl.BlockSpec(memory_space=pltpu.VMEM)
SMEM = pl.BlockSpec(memory_space=pltpu.SMEM)
ANY = pl.BlockSpec(memory_space=pl.ANY)


def passed_along(shard, axis, by):
    length = lax.axis_size(axis)
    pairs = [(i, i + by) for i in range(length) if 0 <= i + by < length]
    return lax.ppermute(shard, axis, pairs)


def split_rows(values):
    high = values.astype(jnp.bfloat16)
    low = (values - high.astype(jnp.float32)).astype(jnp.bfloat16)
    return high, low


def product(stacked, tile_high, tile_low, contract):
    members = stacked.shape[0] // 2
    dims = (((1,), (contract,)), ((), ()))
    first = lax.dot_general(stacked, tile_high, dims, preferred_element_type=jnp.float32)
    second = lax.dot_general(
        stacked[:members], tile_low, dims, preferred_element_type=jnp.float32
    )
    return first[:members] + first[members:] + second


def build_tile(pos_src, src, pos_dst, dst, cls_src, cls_dst, amp_ref, scale_ref, tile_ref):
    size = pos_dst.shape[2]
    columns = [
        jnp.transpose(jnp.broadcast_to(pos_src[axis, pl.ds(src, 1), :], (8, size)))
        for axis in range(2)
    ]
    rows = [pos_dst[axis, pl.ds(dst, 1), :] for axis in range(2)]
    classes = []
    for k in range(amp_ref.shape[1]):
        weight = amp_ref[cls_src, k] * amp_ref[cls_dst, k]
        scale = scale_ref[0, k]
        inv = scale_ref[1, k]
        inv2 = inv * inv
        classes.append(
            (
                scale,
                2.0 * scale,
                -0.5 * scale * scale,
                weight * inv2 * inv2 * inv * (1.0 / 12.0),
                weight,
                weight * inv2 * (-5.0 / 3.0),
                weight * inv2 * inv * 0.625,
                weight * inv2 * inv2 * 0.5,
                weight * inv2 * inv2 * inv * -0.25,
            )
        )
    for start in range(0, size, ROWS):
        part = slice(start, start + ROWS)
        east = columns[0][part, :1] - rows[0]
        north = columns[1][part, :1] - rows[1]
        square = east * east + north * north
        inverse = lax.rsqrt(jnp.maximum(square, 1e-30))
        dist = square * inverse
        total = None
        for scale, twice, shift, out_w, c0, c2, c3, c4, c5 in classes:
            inner = c0 + square * (c2 + dist * (c3 + dist * (c4 + dist * c5)))
            gap = jnp.maximum(twice - dist, 0.0)
            gap = gap * gap
            outer = (gap * gap) * ((square + dist * twice + shift) * (inverse * out_w))
            term = jnp.where(dist <= scale, inner, outer)
            total = term if total is None else total + term
        high, low = split_rows(total)
        tile_ref[0, part, :] = high
        tile_ref[1, part, :] = low


def build_loop(base, count, tiles_ref, slots, sems, make, use):
    def slot_of(t):
        return slots.at[lax.rem(t, SLOTS)]

    def copy(t):
        return pltpu.make_async_copy(slot_of(t), tiles_ref.at[base + t], sems.at[lax.rem(t, SLOTS)])

    @pl.when(count > 0)
    def _():
        make(0, slots.at[0])
        copy(0).start()

    def step(t, carry):
        @pl.when(t >= SLOTS)
        def _():
            copy(t - SLOTS).wait()

        use([(t - 1, slot_of(t - 1))])
        make(t, slot_of(t))
        copy(t).start()
        return carry

    lax.fori_loop(1, count, step, 0)

    @pl.when(count > 0)
    def _():
        use([(count - 1, slot_of(count - 1))])

    def drain(t, carry):
        copy(t).wait()
        return carry

    lax.fori_loop(jnp.maximum(count - SLOTS, 0), count, drain, 0)


def read_loop(base, count, tiles_ref, slots, sems, use):
    groups = lax.div(count + GROUP - 1, GROUP)

    def copy(g):
        slot = lax.rem(g, 2)
        return pltpu.make_async_copy(
            tiles_ref.at[pl.ds(base + g * GROUP, GROUP)], slots.at[slot], sems.at[slot]
        )

    @pl.when(groups > 0)
    def _():
        copy(0).start()

    def step(g, carry):
        @pl.when(g + 1 < groups)
        def _():
            copy(g + 1).start()

        copy(g).wait()
        use([(g * GROUP + j, slots.at[lax.rem(g, 2), j]) for j in range(GROUP)])
        return carry

    lax.fori_loop(0, groups, step, 0)


def stage_values(start, count, base_ref, stacked):
    members = stacked.shape[1] // 2

    def step(b, carry):
        high, low = split_rows(base_ref[b])
        stacked[start + b, :members, :] = high
        stacked[start + b, members:, :] = low
        return carry

    lax.fori_loop(0, count, step, 0)


def add_all(acc, terms):
    for where, term in terms:
        acc[where] += term


def own_kernel(build, entries, *refs):
    if build:
        info, amp, scale, pos, base, tiles, acc, stacked, slots, sems = refs
    else:
        info, base, base_2, tiles, acc, stacked, slots, sems = refs
    live = info[2 * entries + 2]
    count = live + info[2 * entries]
    blocks = stacked.shape[0]
    acc[...] = jnp.zeros_like(acc)
    if build:
        stage_values(0, blocks, base, stacked)
    else:
        stage_values(0, blocks // 2, base, stacked)
        stage_values(blocks // 2, blocks // 2, base_2, stacked)

    def ends(t):
        entry = jnp.clip(t - live, 0, entries - 1)
        src = jnp.where(t < live, t, info[entry])
        dst = jnp.where(t < live, t, info[entries + entry])
        return src, dst

    def make(t, tile):
        src, dst = ends(t)
        first = 2 * entries + 3
        build_tile(pos, src, pos, dst, info[first + src], info[first + dst], amp, scale, tile)

    def use(items):
        terms = []
        for t, tile in items:
            src, dst = ends(t)
            to = jnp.where(t < count, dst, blocks)
            back = jnp.where(jnp.logical_and(t >= live, t < count), src, blocks)
            terms.append((to, product(stacked[src], tile[0], tile[1], 0)))
            terms.append((back, product(stacked[dst], tile[0], tile[1], 1)))
        add_all(acc, terms)

    if build:
        build_loop(0, count, tiles, slots, sems, make, use)
    else:
        read_loop(0, count, tiles, slots, sems, use)


def list_cross(blocks, entries, info, info_s, order):
    local_pairs = info[2 * entries]
    north_pairs = info[2 * entries + 1]
    local_south = info_s[2 * entries]
    count = north_pairs + info_s[2 * entries + 1]

    def ends(t):
        is_north = t < north_pairs
        entry_n = jnp.clip(local_pairs + t, 0, entries - 1)
        entry_s = jnp.clip(local_south + t - north_pairs, 0, entries - 1)
        src = jnp.where(is_north, info[entries + entry_n], blocks + info_s[entry_s])
        return src, jnp.where(is_north, info[entry_n], info_s[entries + entry_s])

    def take(upper):
        def step(t, filled):
            src, dst = ends(t)
            order[filled] = dst * 2 * blocks + src
            mine = (dst >= blocks // 2) if upper else (dst < blocks // 2)
            return filled + mine.astype(jnp.int32)

        return step

    middle = lax.fori_loop(0, count, take(False), 0)
    lax.fori_loop(0, count, take(True), middle)
    order[order.shape[0] - 2] = middle
    order[order.shape[0] - 1] = count


def cross_kernel(build, entries, *refs):
    if build == 1:
        (info, info_n, info_s, amp, scale, pos, pos_two, base_n, base_s, acc_in, sigma, obs_var,
         direct, tiles_in, tiles, image_out, scaled_out, sums, order,
         stacked, slots, sems, acc, parts) = refs
    elif build == 2:
        (info, info_n, info_s, order, amp, scale, pos, pos_two, base_n, base_s, acc_in, sigma, obs_var,
         direct, sums_in, tiles_in, tiles, image_out, scaled_out, sums,
         stacked, slots, sems, acc, parts) = refs
    else:
        (info, info_n, info_s, order, base_n, base_s, base_n2, base_s2, acc_in, sigma, obs_var,
         direct, direct2, sums_in, tiles, image_out, sums, stacked, slots, sems, acc, parts) = refs
    blocks = sigma.shape[0]
    half_blocks = blocks // 2
    if build == 1:
        list_cross(blocks, entries, info, info_s, order)
    middle = order[order.shape[0] - 2]
    count = order[order.shape[0] - 1]
    start, stop = {0: (0, count), 1: (0, middle), 2: (middle, count)}[build]
    low, high = {0: (0, blocks), 1: (0, half_blocks), 2: (half_blocks, blocks)}[build]
    acc[...] = acc_in[...]
    if build:
        stage_values(0, blocks, base_n, stacked)
        stage_values(blocks, blocks, base_s, stacked)
    else:
        for k, base in enumerate((base_n, base_n2, base_s, base_s2)):
            stage_values(k * half_blocks, half_blocks, base, stacked)

    def ends(t):
        code = order[start + t]
        return lax.rem(code, 2 * blocks), lax.div(code, 2 * blocks)

    def make(t, tile):
        src, dst = ends(t)
        first = 2 * entries + 3
        from_n = info_n[first + jnp.minimum(src, blocks - 1)]
        from_s = info_s[first + jnp.maximum(src - blocks, 0)]
        cls_src = jnp.where(src < blocks, from_n, from_s)
        build_tile(pos_two, src, pos, dst, cls_src, info[first + dst], amp, scale, tile)

    def use(items):
        terms = []
        for t, tile in items:
            src, dst = ends(jnp.minimum(t, stop - start - 1))
            to = jnp.where(t < stop - start, dst, blocks)
            terms.append((to, product(stacked[src], tile[0], tile[1], 0)))
        add_all(acc, terms)

    before = info[2 * entries + 2] + info[2 * entries] + start
    if build:
        build_loop(before, stop - start, tiles, slots, sems, make, use)
    else:
        read_loop(before, stop - start, tiles, slots, sems, use)

    parts[...] = jnp.zeros_like(parts)
    half = parts.shape[2]

    def finish(source, at):
        def step(b, carry):
            weight = sigma[pl.ds(b, 1), :]
            direction = source[b - at]
            result = weight * acc[b] + obs_var[pl.ds(b, 1), :] * direction
            image_out[b - low] = result
            if build:
                scaled_out[b - low] = weight * result
            terms = [direction * result]
            if build:
                terms += [direction * direction, result * result]
            for k, term in enumerate(terms):
                parts[k] += term[:, :half] + term[:, half:]
            return carry

        return step

    if build:
        lax.fori_loop(low, high, finish(direct, 0), 0)
    else:
        lax.fori_loop(0, half_blocks, finish(direct, 0), 0)
        lax.fori_loop(half_blocks, blocks, finish(direct2, half_blocks), 0)
    if build == 1:
        sums[...] = jnp.zeros_like(sums)
    else:
        sums[...] = sums_in[...]
    for k in range(3 if build else 1):
        row = k if build else 3
        sums[row : row + 1, :] += jnp.sum(jnp.transpose(parts[k]), axis=0, keepdims=True)


def total_kernel(low, high, value, out, held_low, held_high, send_low, recv_low, send_high, recv_high):
    me = lax.axis_index("reg")
    place_low, place_high = lax.rem(me, low), lax.div(me, low)

    def peer(stage, k):
        if stage == 0:
            return me - place_low + lax.rem(place_low + k, low)
        return lax.rem(place_high + k, high) * low + place_low

    barrier = pltpu.get_barrier_semaphore()
    for stage, size in enumerate((low, high)):
        for k in range(1, size):
            pl.semaphore_signal(
                barrier, inc=1, device_id={"reg": peer(stage, k)}, device_id_type=MESH
            )
    pl.semaphore_wait(barrier, low + high - 2)
    running = value[...]
    for stage, size, place, held, send, recv in (
        (0, low, place_low, held_low, send_low, recv_low),
        (1, high, place_high, held_high, send_high, recv_high),
    ):
        held[0] = running
        copies = []
        for k in range(1, size):
            copy = pltpu.make_async_remote_copy(
                src_ref=held.at[0],
                dst_ref=held.at[k],
                send_sem=send.at[k],
                recv_sem=recv.at[k],
                device_id={"reg": peer(stage, k)},
                device_id_type=MESH,
            )
            copy.start()
            copies.append(copy)
        for copy in copies:
            copy.wait()
        running = held[lax.rem(place, size)]
        for source in range(1, size):
            running = running + held[lax.rem(place - source + size, size)]
    out[...] = running


def total_over(value):
    n = lax.axis_size("reg")
    if n & (n - 1) or n < 4:
        return lax.psum(value, "reg")
    low = 1 << ((n.bit_length() - 1) // 2)
    high = n // low
    semaphores = [
        pltpu.SemaphoreType.DMA((size,)) for size in (low, low, high, high)
    ]
    return pl.pallas_call(
        functools.partial(total_kernel, low, high),
        out_shape=jax.ShapeDtypeStruct(value.shape, value.dtype),
        in_specs=[VMEM],
        out_specs=VMEM,
        scratch_shapes=[
            pltpu.VMEM((low,) + value.shape, value.dtype),
            pltpu.VMEM((high,) + value.shape, value.dtype),
        ]
        + semaphores,
        compiler_params=pltpu.CompilerParams(collective_id=0, has_side_effects=True),
        name="member_sums",
    )(value)


def local(
    obs_value,
    positions,
    sigma,
    obs_var,
    class_amp,
    length_scale,
    block_class,
    block_count,
    pair_list,
    pair_count,
):
    blocks, members, size = obs_value.shape
    entries = pair_list.shape[1]
    info = jnp.concatenate(
        [pair_list[0], pair_list[1], pair_count[:, 0], block_count, block_class]
    )
    width = info.shape[0]
    info_rows = -(-width // size)
    packed = jnp.concatenate(
        [
            positions.reshape(2 * blocks, size),
            jnp.pad(info.astype(jnp.float32), (0, -width % size)).reshape(-1, size),
        ]
    )
    packed = jnp.pad(packed, ((0, -packed.shape[0] % members), (0, 0)))
    packed = packed.reshape(-1, members, size)
    scales = jnp.stack([length_scale, 1.0 / length_scale])

    live = (jnp.arange(blocks, dtype=jnp.int32) < block_count[0]).astype(jnp.float32)
    first_residual = obs_value * live[:, None, None]
    scaled = jnp.concatenate([sigma[:, None, :] * first_residual, packed])
    scaled_n = passed_along(scaled, "reg", -1)
    scaled_s = passed_along(scaled, "reg", 1)

    def unpacked(bundle):
        rows = bundle[blocks:].reshape(-1, size)
        listed = rows[2 * blocks : 2 * blocks + info_rows].reshape(-1)[:width]
        return rows[: 2 * blocks].reshape(2, blocks, size), listed.astype(jnp.int32)

    pos_n, info_n = unpacked(scaled_n)
    pos_s, info_s = unpacked(scaled_s)
    pos_two = jnp.concatenate([pos_n, pos_s], axis=1)

    own_cap = blocks + min(SIDE_MAX, entries)
    cross_cap = 2 * min(SIDE_MAX, entries)
    cap = blocks + entries + min(SIDE_MAX, entries) + GROUP - 1
    array = jax.ShapeDtypeStruct((blocks, members, size), jnp.float32)
    spread_shape = jax.ShapeDtypeStruct((blocks + 1, members, size), jnp.float32)
    sums_shape = jax.ShapeDtypeStruct((8, members), jnp.float32)
    tiles_shape = jax.ShapeDtypeStruct((cap, 2, size, size), jnp.bfloat16)

    def scratch(count, build):
        held = (SLOTS,) if build else (2, GROUP)
        return [
            pltpu.VMEM((count, 2 * members, size), jnp.bfloat16),
            pltpu.VMEM(held + (2, size, size), jnp.bfloat16),
            pltpu.SemaphoreType.DMA((SLOTS if build else 2,)),
        ]

    parts = [
        pltpu.VMEM(spread_shape.shape, jnp.float32),
        pltpu.VMEM((3, members, size // 2), jnp.float32),
    ]
    params = pltpu.CompilerParams(vmem_limit_bytes=VMEM_BYTES)

    def cost(count, build):
        return pl.CostEstimate(
            flops=count * 6 * size * size * members + build * count * 80 * size * size,
            bytes_accessed=count * 4 * size * size,
            transcendentals=build * count * size * size,
        )

    tiles, spread = pl.pallas_call(
        functools.partial(own_kernel, True, entries),
        out_shape=[tiles_shape, spread_shape],
        in_specs=[SMEM, SMEM, SMEM, VMEM, VMEM],
        out_specs=[ANY, VMEM],
        scratch_shapes=scratch(blocks, True),
        compiler_params=params,
        cost_estimate=cost(own_cap, 1),
        name="own_tiles_and_spread",
    )(info, class_amp, scales, positions, scaled)
    half_array = jax.ShapeDtypeStruct((blocks // 2, members, size), jnp.float32)
    order_shape = jax.ShapeDtypeStruct((cross_cap + 3,), jnp.int32)

    tiles, image, scaled_image, sums, order = pl.pallas_call(
        functools.partial(cross_kernel, 1, entries),
        out_shape=[tiles_shape, half_array, half_array, sums_shape, order_shape],
        in_specs=[SMEM] * 5 + [VMEM] * 8 + [ANY],
        out_specs=[ANY, VMEM, VMEM, VMEM, SMEM],
        input_output_aliases={13: 0},
        scratch_shapes=scratch(2 * blocks, True) + parts,
        compiler_params=params,
        cost_estimate=cost(40 * cross_cap, 1),
        name="cross_tiles_and_image_first",
    )(
        info, info_n, info_s, class_amp, scales, positions, pos_two, scaled_n, scaled_s, spread,
        sigma, obs_var, first_residual, tiles,
    )
    image_n = passed_along(scaled_image, "reg", -1)
    image_s = passed_along(scaled_image, "reg", 1)
    tiles, image_2, scaled_image_2, sums = pl.pallas_call(
        functools.partial(cross_kernel, 2, entries),
        out_shape=[tiles_shape, half_array, half_array, sums_shape],
        in_specs=[SMEM] * 6 + [VMEM] * 9 + [ANY],
        out_specs=[ANY, VMEM, VMEM, VMEM],
        input_output_aliases={15: 0},
        scratch_shapes=scratch(2 * blocks, True) + parts,
        compiler_params=params,
        cost_estimate=cost(40 * cross_cap, 1),
        name="cross_tiles_and_image_second",
    )(
        info, info_n, info_s, order, class_amp, scales, positions, pos_two, scaled_n, scaled_s,
        spread, sigma, obs_var, first_residual, sums, tiles,
    )
    scaled_image_2, image_n, image_s = lax.optimization_barrier((scaled_image_2, image_n, image_s))
    image_n2 = passed_along(scaled_image_2, "reg", -1)
    image_s2 = passed_along(scaled_image_2, "reg", 1)
    spread = pl.pallas_call(
        functools.partial(own_kernel, False, entries),
        out_shape=spread_shape,
        in_specs=[SMEM, VMEM, VMEM, ANY],
        out_specs=VMEM,
        scratch_shapes=scratch(blocks, False),
        compiler_params=params,
        cost_estimate=pl.CostEstimate(flops=0, bytes_accessed=0, transcendentals=0),
        name="own_spread",
    )(info, scaled_image, scaled_image_2, tiles)
    second_image, sums = pl.pallas_call(
        functools.partial(cross_kernel, 0, entries),
        out_shape=[array, sums_shape],
        in_specs=[SMEM] * 4 + [VMEM] * 10 + [ANY],
        out_specs=[VMEM, VMEM],
        scratch_shapes=scratch(2 * blocks, False) + parts,
        compiler_params=params,
        cost_estimate=cost(cross_cap, 0),
        name="cross_image",
    )(
        info, info_n, info_s, order, image_n, image_s, image_n2, image_s2, spread, sigma, obs_var,
        image, image_2, sums, tiles,
    )
    image = jnp.concatenate([image, image_2])

    totals = total_over(sums)
    curvature, norm = totals[0], totals[1]
    step = norm / curvature
    norm_next = jnp.maximum(norm - 2.0 * step * curvature + step * step * totals[2], 0.0)
    keep = 1.0 + norm_next / norm
    curvature_next = keep * (keep * curvature - 2.0 * step * totals[2]) + step * step * totals[3]
    step_next = norm_next / curvature_next

    def along(member_values):
        return member_values[None, :, None]

    weights = along(step + step_next * keep) * first_residual - along(step_next * step) * image
    residual = (
        first_residual
        - along(step + step_next * keep) * image
        + along(step_next * step) * second_image
    )
    return (weights, residual)


def solution(mesh):
    placed = (
        P(("grp", "reg"), None, None),
        P(None, ("grp", "reg"), None),
        P(("grp", "reg"), None),
        P(("grp", "reg"), None),
        P(),
        P(),
        P(("grp", "reg")),
        P(("grp", "reg")),
        P(None, ("grp", "reg")),
        P(None, ("grp", "reg")),
    )
    return jax.shard_map(
        local,
        mesh=mesh,
        in_specs=placed,
        out_specs=(P(("grp", "reg"), None, None), P(("grp", "reg"), None, None)),
        check_vma=False,
    )
```

```python
import functools

import jax
import jax.numpy as jnp
from jax import lax
from jax.experimental import pallas as pl
from jax.experimental.pallas import tpu as pltpu
from jax.sharding import PartitionSpec as P

SIDE_MAX = 46
SLOTS = 4
GROUP = 4
ROWS = 16
MESH = pl.DeviceIdType.MESH
VMEM_BYTES = 56 * 1024 * 1024
VMEM = pl.BlockSpec(memory_space=pltpu.VMEM)
SMEM = pl.BlockSpec(memory_space=pltpu.SMEM)
ANY = pl.BlockSpec(memory_space=pl.ANY)


def passed_along(shard, axis, by):
    length = lax.axis_size(axis)
    pairs = [(i, i + by) for i in range(length) if 0 <= i + by < length]
    return lax.ppermute(shard, axis, pairs)


def split_rows(values):
    high = values.astype(jnp.bfloat16)
    low = (values - high.astype(jnp.float32)).astype(jnp.bfloat16)
    return high, low


def product(stacked, tile_high, tile_low, contract):
    members = stacked.shape[0] // 2
    dims = (((1,), (contract,)), ((), ()))
    first = lax.dot_general(stacked, tile_high, dims, preferred_element_type=jnp.float32)
    second = lax.dot_general(
        stacked[:members], tile_low, dims, preferred_element_type=jnp.float32
    )
    return first[:members] + first[members:] + second


def build_tile(
    pos_src, src, pos_dst, dst, cls_src, cls_dst, amp_ref, scale_ref, tile_ref, mirrored=False
):
    size = pos_dst.shape[2]
    half = size // 2
    columns = [
        jnp.transpose(jnp.broadcast_to(pos_src[axis, pl.ds(src, 1), :], (8, size)))
        for axis in range(2)
    ]
    rows = [pos_dst[axis, pl.ds(dst, 1), :] for axis in range(2)]
    classes = []
    for k in range(amp_ref.shape[1]):
        weight = amp_ref[cls_src, k] * amp_ref[cls_dst, k]
        scale = scale_ref[0, k]
        inv = scale_ref[1, k]
        inv2 = inv * inv
        scale2 = scale * scale
        classes.append(
            (
                2.0 * scale,
                2.5 * scale2,
                (20.0 / 3.0) * scale2 * scale,
                12.0 * scale2 * scale2 * scale,
                -0.5 * scale2,
                weight * inv2 * inv2 * inv * (1.0 / 12.0),
            )
        )
    kept = []
    for start in range(0, size, ROWS):
        part = slice(start, start + ROWS)
        first = half if mirrored and start >= half else 0
        east = columns[0][part, :1] - rows[0][:, first:]
        north = columns[1][part, :1] - rows[1][:, first:]
        square = east * east + north * north
        inverse = lax.rsqrt(jnp.maximum(square, 1e-30))
        dist = square * inverse
        twice_square = square + square
        three_square = square * -3.0
        total = None
        for twice, near, cube, fifth, shift, out_w in classes:
            gap = twice - dist
            slope = dist * gap
            inner = fifth + three_square * (cube - dist * (slope + near))
            gap = jnp.maximum(gap, 0.0)
            gap = gap * gap
            outer = (gap * gap) * ((slope + twice_square + shift) * inverse)
            term = jnp.maximum(inner, outer) * out_w
            total = term if total is None else total + term
        high, low = split_rows(total)
        tile_ref[0, part, first:] = high
        tile_ref[1, part, first:] = low
        if mirrored and start < half:
            kept.append(total[:, half:])
    if mirrored:
        high, low = split_rows(jnp.transpose(jnp.concatenate(kept)))
        tile_ref[0, half:, :half] = high
        tile_ref[1, half:, :half] = low


def build_loop(base, count, tiles_ref, slots, sems, make, use):
    def slot_of(t):
        return slots.at[lax.rem(t, SLOTS)]

    def copy(t):
        return pltpu.make_async_copy(slot_of(t), tiles_ref.at[base + t], sems.at[lax.rem(t, SLOTS)])

    @pl.when(count > 0)
    def _():
        make(0, slots.at[0])
        copy(0).start()

    def step(t, carry):
        @pl.when(t >= SLOTS)
        def _():
            copy(t - SLOTS).wait()

        use([(t - 1, slot_of(t - 1))])
        make(t, slot_of(t))
        copy(t).start()
        return carry

    lax.fori_loop(1, count, step, 0)

    @pl.when(count > 0)
    def _():
        use([(count - 1, slot_of(count - 1))])

    def drain(t, carry):
        copy(t).wait()
        return carry

    lax.fori_loop(jnp.maximum(count - SLOTS, 0), count, drain, 0)


def read_loop(base, count, tiles_ref, slots, sems, use):
    groups = lax.div(count + GROUP - 1, GROUP)

    def copy(g):
        slot = lax.rem(g, 2)
        return pltpu.make_async_copy(
            tiles_ref.at[pl.ds(base + g * GROUP, GROUP)], slots.at[slot], sems.at[slot]
        )

    @pl.when(groups > 0)
    def _():
        copy(0).start()

    def step(g, carry):
        @pl.when(g + 1 < groups)
        def _():
            copy(g + 1).start()

        copy(g).wait()
        use([(g * GROUP + j, slots.at[lax.rem(g, 2), j]) for j in range(GROUP)])
        return carry

    lax.fori_loop(0, groups, step, 0)


def stage_values(start, count, base_ref, stacked):
    members = stacked.shape[1] // 2

    def step(b, carry):
        high, low = split_rows(base_ref[b])
        stacked[start + b, :members, :] = high
        stacked[start + b, members:, :] = low
        return carry

    lax.fori_loop(0, count, step, 0)


def add_all(acc, terms):
    for where, term in terms:
        acc[where] += term


def own_kernel(build, entries, *refs):
    if build:
        info, amp, scale, pos, base, tiles, acc, stacked, slots, sems = refs
    else:
        info, base, base_2, tiles, acc, stacked, slots, sems = refs
    live = info[2 * entries + 2]
    count = live + info[2 * entries]
    blocks = stacked.shape[0]
    acc[...] = jnp.zeros_like(acc)
    if build:
        stage_values(0, blocks, base, stacked)
    else:
        stage_values(0, blocks // 2, base, stacked)
        stage_values(blocks // 2, blocks // 2, base_2, stacked)

    def ends(t):
        entry = jnp.clip(t - live, 0, entries - 1)
        src = jnp.where(t < live, t, info[entry])
        dst = jnp.where(t < live, t, info[entries + entry])
        return src, dst

    first = 2 * entries + 3

    def make_diagonal(t, tile):
        build_tile(pos, t, pos, t, info[first + t], info[first + t], amp, scale, tile, True)

    def use_diagonal(items):
        add_all(acc, [(t, product(stacked[t], tile[0], tile[1], 0)) for t, tile in items])

    def make(t, tile):
        src, dst = ends(t + live)
        build_tile(pos, src, pos, dst, info[first + src], info[first + dst], amp, scale, tile)

    def use(items):
        terms = []
        for t, tile in items:
            t = t + live if build else t
            src, dst = ends(t)
            to = jnp.where(t < count, dst, blocks)
            back = jnp.where(jnp.logical_and(t >= live, t < count), src, blocks)
            terms.append((to, product(stacked[src], tile[0], tile[1], 0)))
            terms.append((back, product(stacked[dst], tile[0], tile[1], 1)))
        add_all(acc, terms)

    if build:
        build_loop(0, live, tiles, slots, sems, make_diagonal, use_diagonal)
        build_loop(live, count - live, tiles, slots, sems, make, use)
    else:
        read_loop(0, count, tiles, slots, sems, use)


def list_cross(blocks, entries, info, info_s, order):
    local_pairs = info[2 * entries]
    north_pairs = info[2 * entries + 1]
    local_south = info_s[2 * entries]
    count = north_pairs + info_s[2 * entries + 1]

    def ends(t):
        is_north = t < north_pairs
        entry_n = jnp.clip(local_pairs + t, 0, entries - 1)
        entry_s = jnp.clip(local_south + t - north_pairs, 0, entries - 1)
        src = jnp.where(is_north, info[entries + entry_n], blocks + info_s[entry_s])
        return src, jnp.where(is_north, info[entry_n], info_s[entries + entry_s])

    def take(upper):
        def step(t, filled):
            src, dst = ends(t)
            order[filled] = dst * 2 * blocks + src
            mine = (dst >= blocks // 2) if upper else (dst < blocks // 2)
            return filled + mine.astype(jnp.int32)

        return step

    middle = lax.fori_loop(0, count, take(False), 0)
    lax.fori_loop(0, count, take(True), middle)
    order[order.shape[0] - 2] = middle
    order[order.shape[0] - 1] = count


def cross_kernel(build, entries, *refs):
    if build == 1:
        (info, info_n, info_s, amp, scale, pos, pos_two, base_n, base_s, acc_in, sigma, obs_var,
         direct, tiles_in, tiles, image_out, scaled_out, sums, order,
         stacked, slots, sems, acc, parts) = refs
    elif build == 2:
        (info, info_n, info_s, order, amp, scale, pos, pos_two, base_n, base_s, acc_in, sigma, obs_var,
         direct, sums_in, tiles_in, tiles, image_out, scaled_out, sums,
         stacked, slots, sems, acc, parts) = refs
    else:
        (info, info_n, info_s, order, base_n, base_s, base_n2, base_s2, acc_in, sigma, obs_var,
         direct, direct2, sums_in, tiles, image_out, sums, stacked, slots, sems, acc, parts) = refs
    blocks = sigma.shape[0]
    half_blocks = blocks // 2
    if build == 1:
        list_cross(blocks, entries, info, info_s, order)
    middle = order[order.shape[0] - 2]
    count = order[order.shape[0] - 1]
    start, stop = {0: (0, count), 1: (0, middle), 2: (middle, count)}[build]
    low, high = {0: (0, blocks), 1: (0, half_blocks), 2: (half_blocks, blocks)}[build]
    acc[...] = acc_in[...]
    if build:
        stage_values(0, blocks, base_n, stacked)
        stage_values(blocks, blocks, base_s, stacked)
    else:
        for k, base in enumerate((base_n, base_n2, base_s, base_s2)):
            stage_values(k * half_blocks, half_blocks, base, stacked)

    def ends(t):
        code = order[start + t]
        return lax.rem(code, 2 * blocks), lax.div(code, 2 * blocks)

    def make(t, tile):
        src, dst = ends(t)
        first = 2 * entries + 3
        from_n = info_n[first + jnp.minimum(src, blocks - 1)]
        from_s = info_s[first + jnp.maximum(src - blocks, 0)]
        cls_src = jnp.where(src < blocks, from_n, from_s)
        build_tile(pos_two, src, pos, dst, cls_src, info[first + dst], amp, scale, tile)

    def use(items):
        terms = []
        for t, tile in items:
            src, dst = ends(jnp.minimum(t, stop - start - 1))
            to = jnp.where(t < stop - start, dst, blocks)
            terms.append((to, product(stacked[src], tile[0], tile[1], 0)))
        add_all(acc, terms)

    before = info[2 * entries + 2] + info[2 * entries] + start
    if build:
        build_loop(before, stop - start, tiles, slots, sems, make, use)
    else:
        read_loop(before, stop - start, tiles, slots, sems, use)

    parts[...] = jnp.zeros_like(parts)
    half = parts.shape[2]

    def finish(source, at):
        def step(b, carry):
            weight = sigma[pl.ds(b, 1), :]
            direction = source[b - at]
            result = weight * acc[b] + obs_var[pl.ds(b, 1), :] * direction
            image_out[b - low] = result
            if build:
                scaled_out[b - low] = weight * result
            terms = [direction * result]
            if build:
                terms += [direction * direction, result * result]
            for k, term in enumerate(terms):
                parts[k] += term[:, :half] + term[:, half:]
            return carry

        return step

    if build:
        lax.fori_loop(low, high, finish(direct, 0), 0)
    else:
        lax.fori_loop(0, half_blocks, finish(direct, 0), 0)
        lax.fori_loop(half_blocks, blocks, finish(direct2, half_blocks), 0)
    if build == 1:
        sums[...] = jnp.zeros_like(sums)
    else:
        sums[...] = sums_in[...]
    for k in range(3 if build else 1):
        row = k if build else 3
        sums[row : row + 1, :] += jnp.sum(jnp.transpose(parts[k]), axis=0, keepdims=True)


def total_kernel(low, high, value, out, held_low, held_high, send_low, recv_low, send_high, recv_high):
    me = lax.axis_index("reg")
    place_low, place_high = lax.rem(me, low), lax.div(me, low)

    def peer(stage, k):
        if stage == 0:
            return me - place_low + lax.rem(place_low + k, low)
        return lax.rem(place_high + k, high) * low + place_low

    barrier = pltpu.get_barrier_semaphore()
    for stage, size in enumerate((low, high)):
        for k in range(1, size):
            pl.semaphore_signal(
                barrier, inc=1, device_id={"reg": peer(stage, k)}, device_id_type=MESH
            )
    pl.semaphore_wait(barrier, low + high - 2)
    running = value[...]
    for stage, size, place, held, send, recv in (
        (0, low, place_low, held_low, send_low, recv_low),
        (1, high, place_high, held_high, send_high, recv_high),
    ):
        held[0] = running
        copies = []
        for k in range(1, size):
            copy = pltpu.make_async_remote_copy(
                src_ref=held.at[0],
                dst_ref=held.at[k],
                send_sem=send.at[k],
                recv_sem=recv.at[k],
                device_id={"reg": peer(stage, k)},
                device_id_type=MESH,
            )
            copy.start()
            copies.append(copy)
        for copy in copies:
            copy.wait()
        running = held[lax.rem(place, size)]
        for source in range(1, size):
            running = running + held[lax.rem(place - source + size, size)]
    out[...] = running


def total_over(value):
    n = lax.axis_size("reg")
    if n & (n - 1) or n < 4:
        return lax.psum(value, "reg")
    low = 1 << ((n.bit_length() - 1) // 2)
    high = n // low
    semaphores = [
        pltpu.SemaphoreType.DMA((size,)) for size in (low, low, high, high)
    ]
    return pl.pallas_call(
        functools.partial(total_kernel, low, high),
        out_shape=jax.ShapeDtypeStruct(value.shape, value.dtype),
        in_specs=[VMEM],
        out_specs=VMEM,
        scratch_shapes=[
            pltpu.VMEM((low,) + value.shape, value.dtype),
            pltpu.VMEM((high,) + value.shape, value.dtype),
        ]
        + semaphores,
        compiler_params=pltpu.CompilerParams(collective_id=0, has_side_effects=True),
        name="member_sums",
    )(value)


def local(
    obs_value,
    positions,
    sigma,
    obs_var,
    class_amp,
    length_scale,
    block_class,
    block_count,
    pair_list,
    pair_count,
):
    blocks, members, size = obs_value.shape
    entries = pair_list.shape[1]
    info = jnp.concatenate(
        [pair_list[0], pair_list[1], pair_count[:, 0], block_count, block_class]
    )
    width = info.shape[0]
    info_rows = -(-width // size)
    packed = jnp.concatenate(
        [
            positions.reshape(2 * blocks, size),
            jnp.pad(info.astype(jnp.float32), (0, -width % size)).reshape(-1, size),
        ]
    )
    packed = jnp.pad(packed, ((0, -packed.shape[0] % members), (0, 0)))
    packed = packed.reshape(-1, members, size)
    scales = jnp.stack([length_scale, 1.0 / length_scale])

    live = (jnp.arange(blocks, dtype=jnp.int32) < block_count[0]).astype(jnp.float32)
    first_residual = obs_value * live[:, None, None]
    scaled = jnp.concatenate([sigma[:, None, :] * first_residual, packed])
    scaled_n = passed_along(scaled, "reg", -1)
    scaled_s = passed_along(scaled, "reg", 1)

    def unpacked(bundle):
        rows = bundle[blocks:].reshape(-1, size)
        listed = rows[2 * blocks : 2 * blocks + info_rows].reshape(-1)[:width]
        return rows[: 2 * blocks].reshape(2, blocks, size), listed.astype(jnp.int32)

    pos_n, info_n = unpacked(scaled_n)
    pos_s, info_s = unpacked(scaled_s)
    pos_two = jnp.concatenate([pos_n, pos_s], axis=1)

    own_cap = blocks + min(SIDE_MAX, entries)
    cross_cap = 2 * min(SIDE_MAX, entries)
    cap = blocks + entries + min(SIDE_MAX, entries) + GROUP - 1
    array = jax.ShapeDtypeStruct((blocks, members, size), jnp.float32)
    spread_shape = jax.ShapeDtypeStruct((blocks + 1, members, size), jnp.float32)
    sums_shape = jax.ShapeDtypeStruct((8, members), jnp.float32)
    tiles_shape = jax.ShapeDtypeStruct((cap, 2, size, size), jnp.bfloat16)

    def scratch(count, build):
        held = (SLOTS,) if build else (2, GROUP)
        return [
            pltpu.VMEM((count, 2 * members, size), jnp.bfloat16),
            pltpu.VMEM(held + (2, size, size), jnp.bfloat16),
            pltpu.SemaphoreType.DMA((SLOTS if build else 2,)),
        ]

    parts = [
        pltpu.VMEM(spread_shape.shape, jnp.float32),
        pltpu.VMEM((3, members, size // 2), jnp.float32),
    ]
    params = pltpu.CompilerParams(vmem_limit_bytes=VMEM_BYTES)

    def cost(count, build):
        return pl.CostEstimate(
            flops=count * 6 * size * size * members + build * count * 80 * size * size,
            bytes_accessed=count * 4 * size * size,
            transcendentals=build * count * size * size,
        )

    tiles, spread = pl.pallas_call(
        functools.partial(own_kernel, True, entries),
        out_shape=[tiles_shape, spread_shape],
        in_specs=[SMEM, SMEM, SMEM, VMEM, VMEM],
        out_specs=[ANY, VMEM],
        scratch_shapes=scratch(blocks, True),
        compiler_params=params,
        cost_estimate=cost(own_cap, 1),
        name="own_tiles_and_spread",
    )(info, class_amp, scales, positions, scaled)
    half_array = jax.ShapeDtypeStruct((blocks // 2, members, size), jnp.float32)
    order_shape = jax.ShapeDtypeStruct((cross_cap + 3,), jnp.int32)

    tiles, image, scaled_image, sums, order = pl.pallas_call(
        functools.partial(cross_kernel, 1, entries),
        out_shape=[tiles_shape, half_array, half_array, sums_shape, order_shape],
        in_specs=[SMEM] * 5 + [VMEM] * 8 + [ANY],
        out_specs=[ANY, VMEM, VMEM, VMEM, SMEM],
        input_output_aliases={13: 0},
        scratch_shapes=scratch(2 * blocks, True) + parts,
        compiler_params=params,
        cost_estimate=cost(40 * cross_cap, 1),
        name="cross_tiles_and_image_first",
    )(
        info, info_n, info_s, class_amp, scales, positions, pos_two, scaled_n, scaled_s, spread,
        sigma, obs_var, first_residual, tiles,
    )
    image_n = passed_along(scaled_image, "reg", -1)
    image_s = passed_along(scaled_image, "reg", 1)
    tiles, image_2, scaled_image_2, sums = pl.pallas_call(
        functools.partial(cross_kernel, 2, entries),
        out_shape=[tiles_shape, half_array, half_array, sums_shape],
        in_specs=[SMEM] * 6 + [VMEM] * 9 + [ANY],
        out_specs=[ANY, VMEM, VMEM, VMEM],
        input_output_aliases={15: 0},
        scratch_shapes=scratch(2 * blocks, True) + parts,
        compiler_params=params,
        cost_estimate=cost(40 * cross_cap, 1),
        name="cross_tiles_and_image_second",
    )(
        info, info_n, info_s, order, class_amp, scales, positions, pos_two, scaled_n, scaled_s,
        spread, sigma, obs_var, first_residual, sums, tiles,
    )
    scaled_image_2, image_n, image_s = lax.optimization_barrier((scaled_image_2, image_n, image_s))
    image_n2 = passed_along(scaled_image_2, "reg", -1)
    image_s2 = passed_along(scaled_image_2, "reg", 1)
    spread = pl.pallas_call(
        functools.partial(own_kernel, False, entries),
        out_shape=spread_shape,
        in_specs=[SMEM, VMEM, VMEM, ANY],
        out_specs=VMEM,
        scratch_shapes=scratch(blocks, False),
        compiler_params=params,
        cost_estimate=pl.CostEstimate(flops=0, bytes_accessed=0, transcendentals=0),
        name="own_spread",
    )(info, scaled_image, scaled_image_2, tiles)
    second_image, sums = pl.pallas_call(
        functools.partial(cross_kernel, 0, entries),
        out_shape=[array, sums_shape],
        in_specs=[SMEM] * 4 + [VMEM] * 10 + [ANY],
        out_specs=[VMEM, VMEM],
        scratch_shapes=scratch(2 * blocks, False) + parts,
        compiler_params=params,
        cost_estimate=cost(cross_cap, 0),
        name="cross_image",
    )(
        info, info_n, info_s, order, image_n, image_s, image_n2, image_s2, spread, sigma, obs_var,
        image, image_2, sums, tiles,
    )
    image = jnp.concatenate([image, image_2])

    totals = total_over(sums)
    curvature, norm = totals[0], totals[1]
    step = norm / curvature
    norm_next = jnp.maximum(norm - 2.0 * step * curvature + step * step * totals[2], 0.0)
    keep = 1.0 + norm_next / norm
    curvature_next = keep * (keep * curvature - 2.0 * step * totals[2]) + step * step * totals[3]
    step_next = norm_next / curvature_next

    def along(member_values):
        return member_values[None, :, None]

    weights = along(step + step_next * keep) * first_residual - along(step_next * step) * image
    residual = (
        first_residual
        - along(step + step_next * keep) * image
        + along(step_next * step) * second_image
    )
    return (weights, residual)


def solution(mesh):
    placed = (
        P(("grp", "reg"), None, None),
        P(None, ("grp", "reg"), None),
        P(("grp", "reg"), None),
        P(("grp", "reg"), None),
        P(),
        P(),
        P(("grp", "reg")),
        P(("grp", "reg")),
        P(None, ("grp", "reg")),
        P(None, ("grp", "reg")),
    )
    return jax.shard_map(
        local,
        mesh=mesh,
        in_specs=placed,
        out_specs=(P(("grp", "reg"), None, None), P(("grp", "reg"), None, None)),
        check_vma=False,
    )
```

```python
import functools

import jax
import jax.numpy as jnp
from jax import lax
from jax.experimental import pallas as pl
from jax.experimental.pallas import tpu as pltpu
from jax.sharding import PartitionSpec as P

SIDE_MAX = 46
SLOTS = 4
GROUP = 4
AHEAD = 2
ROWS = 16
MESH = pl.DeviceIdType.MESH
VMEM_BYTES = 56 * 1024 * 1024
VMEM = pl.BlockSpec(memory_space=pltpu.VMEM)
SMEM = pl.BlockSpec(memory_space=pltpu.SMEM)
ANY = pl.BlockSpec(memory_space=pl.ANY)


def passed_along(shard, axis, by):
    length = lax.axis_size(axis)
    pairs = [(i, i + by) for i in range(length) if 0 <= i + by < length]
    return lax.ppermute(shard, axis, pairs)


def split_rows(values):
    high = values.astype(jnp.bfloat16)
    low = (values - high.astype(jnp.float32)).astype(jnp.bfloat16)
    return high, low


def product(stacked, tile_high, tile_low, contract):
    members = stacked.shape[0] // 2
    dims = (((1,), (contract,)), ((), ()))
    first = lax.dot_general(stacked, tile_high, dims, preferred_element_type=jnp.float32)
    second = lax.dot_general(
        stacked[:members], tile_low, dims, preferred_element_type=jnp.float32
    )
    return first[:members] + first[members:] + second


def build_tile(
    pos_src, src, pos_dst, dst, cls_src, cls_dst, amp_ref, scale_ref, tile_ref, mirrored=False
):
    size = pos_dst.shape[2]
    half = size // 2
    columns = [
        jnp.transpose(jnp.broadcast_to(pos_src[axis, pl.ds(src, 1), :], (8, size)))
        for axis in range(2)
    ]
    rows = [pos_dst[axis, pl.ds(dst, 1), :] for axis in range(2)]
    classes = []
    for k in range(amp_ref.shape[1]):
        weight = amp_ref[cls_src, k] * amp_ref[cls_dst, k]
        scale = scale_ref[0, k]
        inv = scale_ref[1, k]
        inv2 = inv * inv
        scale2 = scale * scale
        classes.append(
            (
                2.0 * scale,
                2.5 * scale2,
                (20.0 / 3.0) * scale2 * scale,
                12.0 * scale2 * scale2 * scale,
                -0.5 * scale2,
                weight * inv2 * inv2 * inv * (1.0 / 12.0),
            )
        )
    kept = []
    for start in range(0, size, ROWS):
        part = slice(start, start + ROWS)
        first = half if mirrored and start >= half else 0
        east = columns[0][part, :1] - rows[0][:, first:]
        north = columns[1][part, :1] - rows[1][:, first:]
        square = east * east + north * north
        inverse = lax.rsqrt(jnp.maximum(square, 1e-30))
        dist = square * inverse
        twice_square = square + square
        three_square = square * -3.0
        total = None
        for twice, near, cube, fifth, shift, out_w in classes:
            gap = twice - dist
            slope = dist * gap
            inner = fifth + three_square * (cube - dist * (slope + near))
            gap = jnp.maximum(gap, 0.0)
            gap = gap * gap
            outer = (gap * gap) * ((slope + twice_square + shift) * inverse)
            term = jnp.maximum(inner, outer) * out_w
            total = term if total is None else total + term
        high, low = split_rows(total)
        tile_ref[0, part, first:] = high
        tile_ref[1, part, first:] = low
        if mirrored and start < half:
            kept.append(total[:, half:])
    if mirrored:
        high, low = split_rows(jnp.transpose(jnp.concatenate(kept)))
        tile_ref[0, half:, :half] = high
        tile_ref[1, half:, :half] = low


def build_loop(base, count, tiles_ref, slots, sems, make, use):
    def slot_of(t):
        return slots.at[lax.rem(t, SLOTS)]

    def copy(t):
        return pltpu.make_async_copy(slot_of(t), tiles_ref.at[base + t], sems.at[lax.rem(t, SLOTS)])

    @pl.when(count > 0)
    def _():
        make(0, slots.at[0])
        copy(0).start()

    def step(t, carry):
        @pl.when(t >= SLOTS)
        def _():
            copy(t - SLOTS).wait()

        use([(t - 1, slot_of(t - 1))])
        make(t, slot_of(t))
        copy(t).start()
        return carry

    lax.fori_loop(1, count, step, 0)

    @pl.when(count > 0)
    def _():
        use([(count - 1, slot_of(count - 1))])

    def drain(t, carry):
        copy(t).wait()
        return carry

    lax.fori_loop(jnp.maximum(count - SLOTS, 0), count, drain, 0)


def read_loop(base, count, tiles_ref, slots, sems, use):
    groups = lax.div(count + GROUP - 1, GROUP)

    def copies(g):
        slot = lax.rem(g, AHEAD + 1)
        return [
            pltpu.make_async_copy(
                tiles_ref.at[base + g * GROUP + j], slots.at[slot, j], sems.at[slot, j]
            )
            for j in range(GROUP)
        ]

    def fetch(g, carry):
        for copy in copies(g):
            copy.start()
        return carry

    lax.fori_loop(0, jnp.minimum(groups, AHEAD), fetch, 0)

    def step(g, carry):
        @pl.when(g + AHEAD < groups)
        def _():
            fetch(g + AHEAD, 0)

        for copy in copies(g):
            copy.wait()
        use([(g * GROUP + j, slots.at[lax.rem(g, AHEAD + 1), j]) for j in range(GROUP)])
        return carry

    lax.fori_loop(0, groups, step, 0)


def stage_values(start, count, base_ref, stacked):
    members = stacked.shape[1] // 2

    def step(b, carry):
        high, low = split_rows(base_ref[b])
        stacked[start + b, :members, :] = high
        stacked[start + b, members:, :] = low
        return carry

    lax.fori_loop(0, count, step, 0)


def add_all(acc, terms):
    for where, term in terms:
        acc[where] += term


def own_kernel(build, entries, *refs):
    if build:
        info, amp, scale, pos, base, tiles, acc, stacked, slots, sems = refs
    else:
        info, base, base_2, tiles, acc, stacked, slots, sems = refs
    live = info[2 * entries + 2]
    count = live + info[2 * entries]
    blocks = stacked.shape[0]
    acc[...] = jnp.zeros_like(acc)
    if build:
        stage_values(0, blocks, base, stacked)
    else:
        stage_values(0, blocks // 2, base, stacked)
        stage_values(blocks // 2, blocks // 2, base_2, stacked)

    def ends(t):
        entry = jnp.clip(t - live, 0, entries - 1)
        src = jnp.where(t < live, t, info[entry])
        dst = jnp.where(t < live, t, info[entries + entry])
        return src, dst

    first = 2 * entries + 3

    def make_diagonal(t, tile):
        build_tile(pos, t, pos, t, info[first + t], info[first + t], amp, scale, tile, True)

    def use_diagonal(items):
        add_all(acc, [(t, product(stacked[t], tile[0], tile[1], 0)) for t, tile in items])

    def make(t, tile):
        src, dst = ends(t + live)
        build_tile(pos, src, pos, dst, info[first + src], info[first + dst], amp, scale, tile)

    def use(items):
        terms = []
        for t, tile in items:
            t = t + live if build else t
            src, dst = ends(t)
            to = jnp.where(t < count, dst, blocks)
            back = jnp.where(jnp.logical_and(t >= live, t < count), src, blocks)
            terms.append((to, product(stacked[src], tile[0], tile[1], 0)))
            terms.append((back, product(stacked[dst], tile[0], tile[1], 1)))
        add_all(acc, terms)

    if build:
        build_loop(0, live, tiles, slots, sems, make_diagonal, use_diagonal)
        build_loop(live, count - live, tiles, slots, sems, make, use)
    else:
        read_loop(0, count, tiles, slots, sems, use)


def list_cross(blocks, entries, info, info_s, order):
    local_pairs = info[2 * entries]
    north_pairs = info[2 * entries + 1]
    local_south = info_s[2 * entries]
    count = north_pairs + info_s[2 * entries + 1]

    def ends(t):
        is_north = t < north_pairs
        entry_n = jnp.clip(local_pairs + t, 0, entries - 1)
        entry_s = jnp.clip(local_south + t - north_pairs, 0, entries - 1)
        src = jnp.where(is_north, info[entries + entry_n], blocks + info_s[entry_s])
        return src, jnp.where(is_north, info[entry_n], info_s[entries + entry_s])

    def take(upper):
        def step(t, filled):
            src, dst = ends(t)
            order[filled] = dst * 2 * blocks + src
            mine = (dst >= blocks // 2) if upper else (dst < blocks // 2)
            return filled + mine.astype(jnp.int32)

        return step

    middle = lax.fori_loop(0, count, take(False), 0)
    lax.fori_loop(0, count, take(True), middle)
    order[order.shape[0] - 2] = middle
    order[order.shape[0] - 1] = count


def cross_kernel(build, entries, *refs):
    if build == 1:
        (info, info_n, info_s, amp, scale, pos, pos_two, base_n, base_s, acc_in, sigma, obs_var,
         direct, tiles_in, tiles, image_out, scaled_out, sums, order,
         stacked, slots, sems, acc, parts) = refs
    elif build == 2:
        (info, info_n, info_s, order, amp, scale, pos, pos_two, base_n, base_s, acc_in, sigma, obs_var,
         direct, sums_in, tiles_in, tiles, image_out, scaled_out, sums,
         stacked, slots, sems, acc, parts) = refs
    else:
        (info, info_n, info_s, order, base_n, base_s, base_n2, base_s2, acc_in, sigma, obs_var,
         direct, direct2, sums_in, tiles, image_out, first_out, sums, stacked, slots, sems, acc, parts) = refs
    blocks = sigma.shape[0]
    half_blocks = blocks // 2
    if build == 1:
        list_cross(blocks, entries, info, info_s, order)
    middle = order[order.shape[0] - 2]
    count = order[order.shape[0] - 1]
    start, stop = {0: (0, count), 1: (0, middle), 2: (middle, count)}[build]
    low, high = {0: (0, blocks), 1: (0, half_blocks), 2: (half_blocks, blocks)}[build]
    acc[...] = acc_in[...]
    if build:
        stage_values(0, blocks, base_n, stacked)
        stage_values(blocks, blocks, base_s, stacked)
    else:
        for k, base in enumerate((base_n, base_n2, base_s, base_s2)):
            stage_values(k * half_blocks, half_blocks, base, stacked)

    def ends(t):
        code = order[start + t]
        return lax.rem(code, 2 * blocks), lax.div(code, 2 * blocks)

    def make(t, tile):
        src, dst = ends(t)
        first = 2 * entries + 3
        from_n = info_n[first + jnp.minimum(src, blocks - 1)]
        from_s = info_s[first + jnp.maximum(src - blocks, 0)]
        cls_src = jnp.where(src < blocks, from_n, from_s)
        build_tile(pos_two, src, pos, dst, cls_src, info[first + dst], amp, scale, tile)

    def use(items):
        terms = []
        for t, tile in items:
            src, dst = ends(jnp.minimum(t, stop - start - 1))
            to = jnp.where(t < stop - start, dst, blocks)
            terms.append((to, product(stacked[src], tile[0], tile[1], 0)))
        add_all(acc, terms)

    before = info[2 * entries + 2] + info[2 * entries] + start
    if build:
        build_loop(before, stop - start, tiles, slots, sems, make, use)
    else:
        read_loop(before, stop - start, tiles, slots, sems, use)

    parts[...] = jnp.zeros_like(parts)
    half = parts.shape[2]

    def finish(source, at):
        def step(b, carry):
            weight = sigma[pl.ds(b, 1), :]
            direction = source[b - at]
            result = weight * acc[b] + obs_var[pl.ds(b, 1), :] * direction
            image_out[b - low] = result
            if build:
                scaled_out[b - low] = weight * result
            else:
                first_out[b] = direction
            terms = [direction * result]
            if build:
                terms += [direction * direction, result * result]
            for k, term in enumerate(terms):
                parts[k] += term[:, :half] + term[:, half:]
            return carry

        return step

    if build:
        lax.fori_loop(low, high, finish(direct, 0), 0)
    else:
        lax.fori_loop(0, half_blocks, finish(direct, 0), 0)
        lax.fori_loop(half_blocks, blocks, finish(direct2, half_blocks), 0)
    if build == 1:
        sums[...] = jnp.zeros_like(sums)
    else:
        sums[...] = sums_in[...]
    for k in range(3 if build else 1):
        row = k if build else 3
        sums[row : row + 1, :] += jnp.sum(jnp.transpose(parts[k]), axis=0, keepdims=True)


def total_kernel(low, high, value, out, held_low, held_high, send_low, recv_low, send_high, recv_high):
    me = lax.axis_index("reg")
    place_low, place_high = lax.rem(me, low), lax.div(me, low)

    def peer(stage, k):
        if stage == 0:
            return me - place_low + lax.rem(place_low + k, low)
        return lax.rem(place_high + k, high) * low + place_low

    barrier = pltpu.get_barrier_semaphore()
    for stage, size in enumerate((low, high)):
        for k in range(1, size):
            pl.semaphore_signal(
                barrier, inc=1, device_id={"reg": peer(stage, k)}, device_id_type=MESH
            )
    pl.semaphore_wait(barrier, low + high - 2)
    running = value[...]
    for stage, size, place, held, send, recv in (
        (0, low, place_low, held_low, send_low, recv_low),
        (1, high, place_high, held_high, send_high, recv_high),
    ):
        held[0] = running
        copies = []
        for k in range(1, size):
            copy = pltpu.make_async_remote_copy(
                src_ref=held.at[0],
                dst_ref=held.at[k],
                send_sem=send.at[k],
                recv_sem=recv.at[k],
                device_id={"reg": peer(stage, k)},
                device_id_type=MESH,
            )
            copy.start()
            copies.append(copy)
        for copy in copies:
            copy.wait()
        running = held[lax.rem(place, size)]
        for source in range(1, size):
            running = running + held[lax.rem(place - source + size, size)]
    out[...] = running


def total_over(value):
    n = lax.axis_size("reg")
    if n & (n - 1) or n < 4:
        return lax.psum(value, "reg")
    low = 1 << ((n.bit_length() - 1) // 2)
    high = n // low
    semaphores = [
        pltpu.SemaphoreType.DMA((size,)) for size in (low, low, high, high)
    ]
    return pl.pallas_call(
        functools.partial(total_kernel, low, high),
        out_shape=jax.ShapeDtypeStruct(value.shape, value.dtype),
        in_specs=[VMEM],
        out_specs=VMEM,
        scratch_shapes=[
            pltpu.VMEM((low,) + value.shape, value.dtype),
            pltpu.VMEM((high,) + value.shape, value.dtype),
        ]
        + semaphores,
        compiler_params=pltpu.CompilerParams(collective_id=0, has_side_effects=True),
        name="member_sums",
    )(value)


def local(
    obs_value,
    positions,
    sigma,
    obs_var,
    class_amp,
    length_scale,
    block_class,
    block_count,
    pair_list,
    pair_count,
):
    blocks, members, size = obs_value.shape
    entries = pair_list.shape[1]
    info = jnp.concatenate(
        [pair_list[0], pair_list[1], pair_count[:, 0], block_count, block_class]
    )
    width = info.shape[0]
    info_rows = -(-width // size)
    packed = jnp.concatenate(
        [
            positions.reshape(2 * blocks, size),
            jnp.pad(info.astype(jnp.float32), (0, -width % size)).reshape(-1, size),
        ]
    )
    packed = jnp.pad(packed, ((0, -packed.shape[0] % members), (0, 0)))
    packed = packed.reshape(-1, members, size)
    scales = jnp.stack([length_scale, 1.0 / length_scale])

    live = (jnp.arange(blocks, dtype=jnp.int32) < block_count[0]).astype(jnp.float32)
    first_residual = obs_value * live[:, None, None]
    scaled = jnp.concatenate([sigma[:, None, :] * first_residual, packed])
    scaled_n = passed_along(scaled, "reg", -1)
    scaled_s = passed_along(scaled, "reg", 1)

    def unpacked(bundle):
        rows = bundle[blocks:].reshape(-1, size)
        listed = rows[2 * blocks : 2 * blocks + info_rows].reshape(-1)[:width]
        return rows[: 2 * blocks].reshape(2, blocks, size), listed.astype(jnp.int32)

    pos_n, info_n = unpacked(scaled_n)
    pos_s, info_s = unpacked(scaled_s)
    pos_two = jnp.concatenate([pos_n, pos_s], axis=1)

    own_cap = blocks + min(SIDE_MAX, entries)
    cross_cap = 2 * min(SIDE_MAX, entries)
    cap = blocks + entries + min(SIDE_MAX, entries) + GROUP - 1
    array = jax.ShapeDtypeStruct((blocks, members, size), jnp.float32)
    spread_shape = jax.ShapeDtypeStruct((blocks + 1, members, size), jnp.float32)
    sums_shape = jax.ShapeDtypeStruct((8, members), jnp.float32)
    tiles_shape = jax.ShapeDtypeStruct((cap, 2, size, size), jnp.bfloat16)

    def scratch(count, build):
        held = (SLOTS,) if build else (AHEAD + 1, GROUP)
        return [
            pltpu.VMEM((count, 2 * members, size), jnp.bfloat16),
            pltpu.VMEM(held + (2, size, size), jnp.bfloat16),
            pltpu.SemaphoreType.DMA(held),
        ]

    parts = [
        pltpu.VMEM(spread_shape.shape, jnp.float32),
        pltpu.VMEM((3, members, size // 2), jnp.float32),
    ]
    params = pltpu.CompilerParams(vmem_limit_bytes=VMEM_BYTES)

    def cost(count, build):
        return pl.CostEstimate(
            flops=count * 6 * size * size * members + build * count * 80 * size * size,
            bytes_accessed=count * 4 * size * size,
            transcendentals=build * count * size * size,
        )

    tiles, spread = pl.pallas_call(
        functools.partial(own_kernel, True, entries),
        out_shape=[tiles_shape, spread_shape],
        in_specs=[SMEM, SMEM, SMEM, VMEM, VMEM],
        out_specs=[ANY, VMEM],
        scratch_shapes=scratch(blocks, True),
        compiler_params=params,
        cost_estimate=cost(own_cap, 1),
        name="own_tiles_and_spread",
    )(info, class_amp, scales, positions, scaled)
    half_array = jax.ShapeDtypeStruct((blocks // 2, members, size), jnp.float32)
    order_shape = jax.ShapeDtypeStruct((cross_cap + 3,), jnp.int32)

    tiles, image, scaled_image, sums, order = pl.pallas_call(
        functools.partial(cross_kernel, 1, entries),
        out_shape=[tiles_shape, half_array, half_array, sums_shape, order_shape],
        in_specs=[SMEM] * 5 + [VMEM] * 8 + [ANY],
        out_specs=[ANY, VMEM, VMEM, VMEM, SMEM],
        input_output_aliases={13: 0},
        scratch_shapes=scratch(2 * blocks, True) + parts,
        compiler_params=params,
        cost_estimate=cost(40 * cross_cap, 1),
        name="cross_tiles_and_image_first",
    )(
        info, info_n, info_s, class_amp, scales, positions, pos_two, scaled_n, scaled_s, spread,
        sigma, obs_var, first_residual, tiles,
    )
    image_n = passed_along(scaled_image, "reg", -1)
    image_s = passed_along(scaled_image, "reg", 1)
    tiles, image_2, scaled_image_2, sums = pl.pallas_call(
        functools.partial(cross_kernel, 2, entries),
        out_shape=[tiles_shape, half_array, half_array, sums_shape],
        in_specs=[SMEM] * 6 + [VMEM] * 9 + [ANY],
        out_specs=[ANY, VMEM, VMEM, VMEM],
        input_output_aliases={15: 0},
        scratch_shapes=scratch(2 * blocks, True) + parts,
        compiler_params=params,
        cost_estimate=cost(40 * cross_cap, 1),
        name="cross_tiles_and_image_second",
    )(
        info, info_n, info_s, order, class_amp, scales, positions, pos_two, scaled_n, scaled_s,
        spread, sigma, obs_var, first_residual, sums, tiles,
    )
    scaled_image_2, image_n, image_s = lax.optimization_barrier((scaled_image_2, image_n, image_s))
    image_n2 = passed_along(scaled_image_2, "reg", -1)
    image_s2 = passed_along(scaled_image_2, "reg", 1)
    spread = pl.pallas_call(
        functools.partial(own_kernel, False, entries),
        out_shape=spread_shape,
        in_specs=[SMEM, VMEM, VMEM, ANY],
        out_specs=VMEM,
        scratch_shapes=scratch(blocks, False),
        compiler_params=params,
        cost_estimate=pl.CostEstimate(flops=0, bytes_accessed=0, transcendentals=0),
        name="own_spread",
    )(info, scaled_image, scaled_image_2, tiles)
    second_image, image, sums = pl.pallas_call(
        functools.partial(cross_kernel, 0, entries),
        out_shape=[array, array, sums_shape],
        in_specs=[SMEM] * 4 + [VMEM] * 10 + [ANY],
        out_specs=[VMEM, VMEM, VMEM],
        scratch_shapes=scratch(2 * blocks, False) + parts,
        compiler_params=params,
        cost_estimate=cost(cross_cap, 0),
        name="cross_image",
    )(
        info, info_n, info_s, order, image_n, image_s, image_n2, image_s2, spread, sigma, obs_var,
        image, image_2, sums, tiles,
    )

    totals = total_over(sums)
    curvature, norm = totals[0], totals[1]
    step = norm / curvature
    norm_next = jnp.maximum(norm - 2.0 * step * curvature + step * step * totals[2], 0.0)
    keep = 1.0 + norm_next / norm
    curvature_next = keep * (keep * curvature - 2.0 * step * totals[2]) + step * step * totals[3]
    step_next = norm_next / curvature_next

    def along(member_values):
        return member_values[None, :, None]

    weights = along(step + step_next * keep) * first_residual - along(step_next * step) * image
    residual = (
        first_residual
        - along(step + step_next * keep) * image
        + along(step_next * step) * second_image
    )
    return (weights, residual)


def solution(mesh):
    placed = (
        P(("grp", "reg"), None, None),
        P(None, ("grp", "reg"), None),
        P(("grp", "reg"), None),
        P(("grp", "reg"), None),
        P(),
        P(),
        P(("grp", "reg")),
        P(("grp", "reg")),
        P(None, ("grp", "reg")),
        P(None, ("grp", "reg")),
    )
    return jax.shard_map(
        local,
        mesh=mesh,
        in_specs=placed,
        out_specs=(P(("grp", "reg"), None, None), P(("grp", "reg"), None, None)),
        check_vma=False,
    )
```
